32 devices in a mesh: ang: 8 (over z, x), sy: 2 (over y), sx: 2 (over core).
Axes of the slice: x: 2, y: 2, z: 4, core: 2. Of those that a mesh axis runs over, the one named last changes fastest.
Arguments:
- objects: bfloat16 [8, 2, 1024, 1024], P('ang', None, 'sy', 'sx'), may hold values from -4 to 4
- probe: float32 [2, 2, 256, 256], replicated, may hold values from -4 to 4
- data: bfloat16 [8, 2, 2, 2, 256, 256], P('ang', 'sy', 'sx'), may hold values from 0 to 4
- positions: int32 [8, 2, 2, 2, 2], P('ang', 'sy', 'sx'), may hold values from 0 to 384
- block_index: int32 [8, 16], replicated, may hold values from 0 to 63, as said below
- block_values: bfloat16 [8, 16, 128, 128], replicated, may hold values from -0.125 to 0.125
Outputs:
- object_grad: float32 [8, 2, 1024, 1024], P('ang', None, 'sy', 'sx')
- probe_grad: float32 [8, 2, 2, 256, 256], P('ang')
- vol_grad: float32 [2, 512, 2, 1024], P('sy', ('ang', 'sx'))
The draws below stay inside these ranges and needn't reach their ends.
Inputs may be any that keep to these rules, and one draw needn't show every extreme that they name: `positions`: A position counts cells from 64 cells before the tile's first row or column. `block_index`: entry g names the angle g // 8 and the column block g % 8; every angle is named by exactly 16 entries.
All inputs are finite; a program needn't handle non-finite values.
Results may differ from the reference program's by a relative error of at most 0.011.
Values may be sent and summed in bfloat16 or wider, within the bound.
No kernel may reach another device: no remote copies, remote signals or barrier semaphores. Data moves between devices by JAX's collectives and lax.ppermute only.
A program may use at most 64 MiB of HBM per device.

```python
import math
from functools import partial
import jax
import jax.numpy as jnp
from jax import lax

PATCH = 256
MODES = 2
TILE = 512
RIM = 64
PATCH_DEV = 2
BLK = 128
KBLK = 16
ANGLES = 8
YTILES = 2
XTILES = 2
OROWS = 1024
W = 1024
LINEB = 8


def draw_block_index(key, part):
    entries = LINEB * KBLK
    ranking = jax.random.permutation(jax.random.fold_in(key, 101), entries)
    angle_of = ranking % ANGLES
    column_of = jax.random.randint(jax.random.fold_in(key, 102), (entries,), 0, LINEB)
    column_of = jnp.where(ranking == entries - 1, LINEB - 1, column_of)
    column_of = jnp.where(ranking == 0, 0, column_of)
    return (angle_of * LINEB + column_of).astype(jnp.int32).reshape(LINEB, KBLK)


def plant(values, key, least, top_value):
    longest = values.shape.index(max(values.shape))
    spots = []
    for shift in (0, 1):
        where = [jax.random.randint(jax.random.fold_in(key, axis), (), 0, length) for axis, length in enumerate(values.shape)]
        where[longest] = (where[longest] + shift) % values.shape[longest]
        spots.append(tuple(where))
    return values.at[spots[0]].set(least).at[spots[1]].set(top_value)


def block_levels(stream_key, extent, pieces, low, high):
    def one(dim, shards_of):
        draws = jax.random.uniform(jax.random.fold_in(jax.random.fold_in(stream_key, 6), dim), (shards_of,), jnp.float32, low / len(pieces), high / len(pieces))
        return jnp.repeat(jnp.exp(draws), extent[dim] // shards_of).reshape((-1,) + (1,) * (len(extent) - dim - 1))

    factor_of = one(*pieces[0])
    for cut in pieces[1:]:
        factor_of = factor_of * one(*cut)
    return factor_of


def normal_values(stream_key, extent, deviation, limit, split=(), kind=jnp.bfloat16):
    gain = block_levels(stream_key, extent, split, -0.22, 0.18) if split else 1.0
    values = jax.random.normal(stream_key, extent, jnp.float32) * deviation * gain
    return jnp.minimum(jnp.maximum(values, -limit), limit).astype(kind)


def setup_inputs(seed: int = 0) -> dict:
    keys = jax.random.split(jax.random.key(seed), 7)
    objects = normal_values(keys[0], (ANGLES, 2, OROWS, W), 0.7, 4.0, ((0, 8), (2, 2), (3, 2)))
    probe = normal_values(keys[1], (MODES, 2, PATCH, PATCH), 0.7, 4.0, (), jnp.float32)
    data = jnp.clip(4.0 * jax.random.uniform(keys[2], (ANGLES, YTILES, XTILES, PATCH_DEV, PATCH, PATCH), jnp.float32) ** block_levels(keys[2], (ANGLES, YTILES, XTILES, PATCH_DEV, PATCH, PATCH), ((0, 8), (1, 2), (2, 2)), -0.2, 0.2), 0.0, 4.0).astype(jnp.bfloat16)
    positions = plant(jax.random.randint(keys[3], (ANGLES, YTILES, XTILES, PATCH_DEV, 2), 0, TILE + 2 * RIM - PATCH + 1), jax.random.fold_in(keys[3], 1), 0, TILE + 2 * RIM - PATCH).astype(jnp.int32)
    block_index = draw_block_index(jax.random.fold_in(keys[6], 71), 0)
    block_values = normal_values(keys[5], (LINEB, KBLK, BLK, BLK), (KBLK * BLK) ** -0.5, 0.125)
    return dict(objects=objects, probe=probe, data=data, positions=positions, block_index=block_index, block_values=block_values)


def dft_parts(length):
    sample_ids = jnp.arange(length, dtype=jnp.int32)
    product = sample_ids[:, None] * sample_ids[None, :] % length
    phases = product.astype(jnp.float32) * (2.0 * math.pi / length)
    factor = 1.0 / math.sqrt(length)
    return (jnp.cos(phases) * factor, -jnp.sin(phases) * factor)

def dft_blocks(length):
    real_part, imag_part = dft_parts(length)
    forward = jnp.stack([jnp.stack([real_part, -imag_part], 1), jnp.stack([imag_part, real_part], 1)], 0)
    backward = jnp.stack([jnp.stack([real_part, imag_part], 1), jnp.stack([-imag_part, real_part], 1)], 0)
    return (forward.astype(jnp.bfloat16), backward.astype(jnp.bfloat16))

def ramp_table(width):
    column_ids = jnp.arange(width, dtype=jnp.int32)
    offsets = column_ids[None, :] - column_ids[:, None]
    odd_cells = offsets % 2 != 0
    scaled = offsets.astype(jnp.float32) * math.pi
    values = jnp.where(odd_cells, -1.0 / jnp.maximum(scaled * scaled, 1.0), 0.0)
    values = jnp.where(offsets == 0, 0.25, values)
    return values.astype(jnp.bfloat16)

def left_product(matrix, fields):
    return jnp.einsum('srtk,btkc->bsrc', matrix.astype(jnp.float32), fields.astype(jnp.float32))

def right_product(fields, matrix):
    return jnp.einsum('btrc,tcsq->bsrq', fields.astype(jnp.float32), matrix.astype(jnp.float32))

def cut_window(field, corner):
    return lax.dynamic_slice(field, (jnp.int32(0), corner[0], corner[1]), (field.shape[0], PATCH, PATCH))

def patch_gradients(patches, measured, probe, forward, backward):
    patch_count = patches.shape[0]
    mode_count = probe.shape[0]
    side = patches.shape[2]
    object_real = patches[:, 0].astype(jnp.float32)[:, None]
    object_imag = patches[:, 1].astype(jnp.float32)[:, None]
    probe_real = probe[None, :, 0]
    probe_imag = probe[None, :, 1]
    exit_real = probe_real * object_real - probe_imag * object_imag
    exit_imag = probe_real * object_imag + probe_imag * object_real
    exit_waves = jnp.stack([exit_real, exit_imag], 2).reshape(patch_count * mode_count, 2, side, side).astype(jnp.bfloat16)
    half_done = left_product(forward, exit_waves).astype(jnp.bfloat16)
    far_field = right_product(half_done, backward).reshape(patch_count, mode_count, 2, side, side)
    intensity = lax.optimization_barrier(jnp.sum(far_field * far_field, axis=(1, 2)))
    misfit = intensity - measured.astype(jnp.float32)
    weighted = (misfit[:, None, None] * far_field).reshape(patch_count * mode_count, 2, side, side).astype(jnp.bfloat16)
    back_half = left_product(backward, weighted).astype(jnp.bfloat16)
    spread = right_product(back_half, forward).reshape(patch_count, mode_count, 2, side, side)
    chi_real = spread[:, :, 0]
    chi_imag = spread[:, :, 1]
    grad_real = lax.optimization_barrier(jnp.sum(probe_real * chi_real + probe_imag * chi_imag, axis=1))
    grad_imag = lax.optimization_barrier(jnp.sum(probe_real * chi_imag - probe_imag * chi_real, axis=1))
    patch_grad = jnp.stack([grad_real, grad_imag], 1)
    probe_real_part = lax.optimization_barrier(jnp.sum(object_real * chi_real + object_imag * chi_imag, axis=0))
    probe_imag_part = lax.optimization_barrier(jnp.sum(object_real * chi_imag - object_imag * chi_real, axis=0))
    probe_part = jnp.stack([probe_real_part, probe_imag_part], 1)
    return (patch_grad, probe_part)

def reference(objects, probe, data, positions, block_index, block_values):
    forward, backward = dft_blocks(PATCH)
    ramp_matrix = ramp_table(W)

    def per_angle(inputs):
        object_angle, data_angle, place_angle = inputs
        padded = jnp.pad(object_angle, ((0, 0), (RIM, RIM), (RIM, RIM)))
        row_base = jnp.arange(YTILES, dtype=jnp.int32)[:, None, None] * TILE
        col_base = jnp.arange(XTILES, dtype=jnp.int32)[None, :, None] * TILE
        row_start = (place_angle[..., 0] + row_base).reshape(-1).astype(jnp.int32)
        col_start = (place_angle[..., 1] + col_base).reshape(-1).astype(jnp.int32)
        starts = jnp.stack([row_start, col_start], 1)
        patches = jax.vmap(partial(cut_window, padded))(starts)
        measured = data_angle.reshape(-1, PATCH, PATCH)
        patch_grad, probe_part = patch_gradients(patches, measured, probe, forward, backward)

        def add_patch(number, current_sum):
            corner = (jnp.int32(0), starts[number, 0], starts[number, 1])
            window = lax.dynamic_slice(current_sum, corner, (2, PATCH, PATCH))
            return lax.dynamic_update_slice(current_sum, window + patch_grad[number], corner)
        running_sum = lax.fori_loop(0, starts.shape[0], add_patch, jnp.zeros(padded.shape, jnp.float32))
        grad_angle = running_sum[:, RIM:RIM + OROWS, RIM:RIM + W]
        sinogram = grad_angle.astype(jnp.bfloat16)
        filtered = jnp.dot(sinogram.reshape(-1, W), ramp_matrix, preferred_element_type=jnp.float32)
        filtered = filtered.reshape(sinogram.shape).astype(jnp.bfloat16)
        return (grad_angle, probe_part, filtered)
    object_grad, probe_parts, filtered_all = lax.map(per_angle, (objects, data, positions))
    probe_grad = probe_parts / math.sqrt(YTILES * XTILES * PATCH_DEV)
    line_data = filtered_all.reshape(ANGLES, 2, OROWS, LINEB, BLK)
    angle_of = block_index // LINEB
    column_of = block_index % LINEB
    picked = line_data[angle_of, :, :, column_of, :]
    volume = jnp.einsum('bkcru,bkuv->rcbv', picked.astype(jnp.float32), block_values.astype(jnp.float32))
    vol_grad = volume.reshape(YTILES, TILE, 2, W)
    return (object_grad, probe_grad, vol_grad)
```

```python
from functools import partial
import math

import jax
import jax.numpy as jnp
import ml_dtypes
import numpy as np
from jax import lax
from jax.experimental import pallas as pl
from jax.experimental.pallas import tpu as pltpu
from jax.sharding import PartitionSpec as P

PATCH = 256
RIM = 64
BLK = 128
SWAP = [(0, 1), (1, 0)]
CROSS = [(0, 3), (3, 0), (1, 2), (2, 1)]
MIB = 1 << 20

VMEM = pl.BlockSpec(memory_space=pltpu.VMEM)
SMEM = pl.BlockSpec(memory_space=pltpu.SMEM)
HBM = pl.BlockSpec(memory_space=pl.ANY)


def dft_blocks(length):
    ids = np.arange(length)
    phases = (ids[:, None] * ids[None, :] % length) * (2.0 * math.pi / length)
    factor = 1.0 / math.sqrt(length)
    re, im = np.cos(phases) * factor, -np.sin(phases) * factor
    forward = np.block([[re, -im], [im, re]])
    backward = np.block([[re, im], [-im, re]])
    return np.stack([forward, backward]).astype(np.float32).astype(ml_dtypes.bfloat16)


def ramp_table(width):
    ids = np.arange(width)
    offsets = ids[None, :] - ids[:, None]
    scaled = offsets.astype(np.float64) * math.pi
    values = np.where(offsets % 2 != 0, -1.0 / np.maximum(scaled * scaled, 1.0), 0.0)
    values = np.where(offsets == 0, 0.25, values)
    return values.astype(np.float32).astype(ml_dtypes.bfloat16)


def shape(dims, dtype=jnp.bfloat16):
    return jax.ShapeDtypeStruct(dims, dtype)


def call(kernel, outs, ins, specs, scratch=(), limit=32, flops=0, moved=0):
    return pl.pallas_call(
        kernel,
        out_shape=outs,
        in_specs=specs,
        out_specs=jax.tree.map(lambda _: VMEM, outs),
        scratch_shapes=list(scratch),
        compiler_params=pltpu.CompilerParams(vmem_limit_bytes=limit * MIB),
        cost_estimate=pl.CostEstimate(flops=flops, bytes_accessed=moved, transcendentals=0),
    )(*ins)


def aligned(value, step):
    return pl.multiple_of(value, step)


def edge_kernel(obj, to_y, to_x, to_d):
    sy, sx = lax.axis_index("sy"), lax.axis_index("sx")
    rows, cols = obj.shape[1], obj.shape[2]
    r = aligned((1 - sy) * (rows - RIM), RIM)
    c = aligned((1 - sx) * (cols - BLK), BLK)
    to_y[...] = obj[:, pl.ds(r, RIM), :]
    to_x[...] = obj[:, :, pl.ds(c, BLK)]
    to_d[...] = obj[:, pl.ds(r, RIM), pl.ds(c, BLK)]


def weight_kernel(count, index, values, ramp, out, total, found):
    me = lax.axis_index("ang")
    lines, per = index.shape
    total[...] = jnp.zeros_like(total)

    def scan(e, n):
        hit = index[e // per, e % per] // lines == me

        @pl.when(hit & (n < count))
        def _():
            found[n] = e

        return n + hit.astype(jnp.int32)

    lax.fori_loop(0, lines * per, scan, jnp.int32(0))

    def add(i, carry):
        e = found[i]
        b, k = e // per, e % per
        col = aligned(index[b, k] % lines * BLK, BLK)
        to = aligned(b * BLK, BLK)
        total[:, pl.ds(to, BLK)] += jnp.dot(
            ramp[:, pl.ds(col, BLK)], values[b, k], preferred_element_type=jnp.float32
        )
        return carry

    lax.fori_loop(0, count, add, 0)
    out[...] = total[...].astype(out.dtype)


def strip_select(half, rows, h, dtype):
    i = lax.broadcasted_iota(jnp.int32, (rows // 2, rows), 0)
    j = lax.broadcasted_iota(jnp.int32, (rows // 2, rows), 1)
    return (j == i // h * 2 * h + half * h + i % h).astype(dtype)


def pick_strips(ref, c, row, rows, lanes, half, h):
    if h % 8 == 0:
        parts = [
            ref[c, pl.ds(aligned(row + q * 2 * h + half * h, 8), h), lanes]
            for q in range(rows // (2 * h))
        ]
        return jnp.concatenate(parts, axis=0).astype(jnp.bfloat16)
    whole = ref[c, pl.ds(aligned(row, 8), rows), lanes].astype(jnp.bfloat16)
    chosen = strip_select(half, rows, h, jnp.bfloat16)
    return jnp.dot(chosen, whole, preferred_element_type=jnp.float32).astype(jnp.bfloat16)


def add_strips(ref, c, row, rows, lanes, half, h, terms):
    if h % 8 == 0:
        for q in range(rows // (2 * h)):
            at = pl.ds(aligned(row + q * 2 * h + half * h, 8), h)
            ref[c, at, lanes] += terms[q * h : (q + 1) * h]
        return
    chosen = strip_select(half, rows, h, jnp.float32)
    at = pl.ds(aligned(row, 8), rows)
    ref[c, at, lanes] += lax.dot_general(
        chosen, terms, (((0,), (0,)), ((), ())), precision=lax.Precision.HIGHEST,
        preferred_element_type=jnp.float32,
    )


def rows_from(value, shift):
    rows, lanes = value.shape[0] - 8, value.shape[1]
    turned = pltpu.roll(value.reshape(rows // 8 + 1, 8, lanes), (8 - shift) % 8, 1)
    keep = lax.broadcasted_iota(jnp.int32, (rows // 8, 8, lanes), 1) < 8 - shift
    return jnp.where(keep, turned[:-1], turned[1:]).reshape(rows, lanes)


def rows_to(value, shift):
    rows, lanes = value.shape
    turned = pltpu.roll(value.reshape(rows // 8, 8, lanes), shift, 1)
    none = jnp.zeros((1, 8, lanes), value.dtype)
    keep = lax.broadcasted_iota(jnp.int32, (rows // 8 + 1, 8, lanes), 1) >= shift
    here = jnp.concatenate([turned, none], axis=0)
    before = jnp.concatenate([none, turned], axis=0)
    return jnp.where(keep, here, before).reshape(rows + 8, lanes)


def patch_kernel(
    h, pos, obj, from_y, from_x, from_d, probe, data, dft,
    grad, own, to_x, rim_x, to_y, to_d, probe_keep, probe_send,
    frame, total, stack, probe_total,
):
    sy, sx = lax.axis_index("sy"), lax.axis_index("sx")
    rows, cols = obj.shape[1], obj.shape[2]
    modes = probe.shape[0]
    patches = data.shape[0]
    f32, bf16 = jnp.float32, jnp.bfloat16
    last = RIM + rows
    row_in = aligned((1 - sy) * last, RIM)
    row_out = aligned(sy * last, RIM)
    col_in = aligned((1 - sx) * (BLK + cols), BLK)
    col_out = aligned(sx * (BLK + cols), BLK)
    inner = pl.ds(BLK, cols)
    for c in range(2):
        frame[c, RIM:last, BLK : BLK + cols] = obj[c].astype(f32)
        frame[c, pl.ds(row_out, RIM), :] = jnp.zeros((RIM, frame.shape[2]), f32)
        frame[c, :, pl.ds(col_out, BLK)] = jnp.zeros((frame.shape[1], BLK), f32)
        frame[c, RIM:last, pl.ds(col_in, BLK)] = from_x[c].astype(f32)
        frame[c, pl.ds(row_in, RIM), inner] = from_y[c].astype(f32)
        frame[c, pl.ds(row_in, RIM), pl.ds(col_in, BLK)] = from_d[c].astype(f32)
    total[...] = jnp.zeros_like(total)
    lane = lax.broadcasted_iota(jnp.int32, (PATCH, BLK), 1)
    spans = PATCH // BLK

    def place(p):
        u, v = pos[p, 0], pos[p, 1] + (BLK - RIM)
        start = aligned(v // BLK * BLK, BLK)
        top = aligned(u // 8 * 8, 8)
        return top, u - top, start, v - start

    def window(p):
        top, down, start, shift = place(p)
        out = []
        for c in range(2):
            cuts = [frame[c, pl.ds(top, PATCH + 8), pl.ds(aligned(start + k * BLK, BLK), BLK)] for k in range(spans + 1)]
            blocks = [pltpu.roll(rows_from(cut, down), (BLK - shift) % BLK, 1) for cut in cuts]
            keep = lane < BLK - shift
            out.append(
                jnp.concatenate([jnp.where(keep, blocks[k], blocks[k + 1]) for k in range(spans)], axis=1)
            )
        return out

    windows = [window(p) for p in range(patches)]
    for p in range(patches):
        o_re, o_im = windows[p]
        for m in range(modes):
            p_re, p_im = probe[m, 0], probe[m, 1]
            at = slice((p * modes + m) * PATCH, (p * modes + m + 1) * PATCH)
            stack[0:PATCH, at] = (p_re * o_re - p_im * o_im).astype(bf16)
            stack[PATCH:, at] = (p_re * o_im + p_im * o_re).astype(bf16)

    def transform(left, right, p):
        at = slice(p * modes * PATCH, (p + 1) * modes * PATCH)
        half = jnp.dot(dft[left], stack[:, at], preferred_element_type=f32).astype(bf16)
        out = []
        for m in range(modes):
            cut = slice(m * PATCH, (m + 1) * PATCH)
            wide = jnp.concatenate([half[:PATCH, cut], half[PATCH:, cut]], axis=1)
            out.append(jnp.dot(wide, dft[right], preferred_element_type=f32))
        return out

    for p in range(patches):
        far = transform(0, 1, p)
        misfit = sum(f[:, :PATCH] * f[:, :PATCH] + f[:, PATCH:] * f[:, PATCH:] for f in far)
        misfit = misfit - data[p].astype(f32)
        for m in range(modes):
            at = slice((p * modes + m) * PATCH, (p * modes + m + 1) * PATCH)
            stack[0:PATCH, at] = (misfit * far[m][:, :PATCH]).astype(bf16)
            stack[PATCH:, at] = (misfit * far[m][:, PATCH:]).astype(bf16)

    for p in range(patches):
        chi = transform(1, 0, p)
        o_re, o_im = windows[p]
        g_re = g_im = 0.0
        for m in range(modes):
            c_re, c_im = chi[m][:, :PATCH], chi[m][:, PATCH:]
            p_re, p_im = probe[m, 0], probe[m, 1]
            g_re += p_re * c_re + p_im * c_im
            g_im += p_re * c_im - p_im * c_re
            q_re, q_im = o_re * c_re + o_im * c_im, o_re * c_im - o_im * c_re
            if p == 0:
                probe_total[m, 0], probe_total[m, 1] = q_re, q_im
            else:
                probe_total[m, 0] += q_re
                probe_total[m, 1] += q_im
        top, down, start, shift = place(p)
        for c, g in enumerate((g_re, g_im)):
            turned = [pltpu.roll(g[:, k * BLK : (k + 1) * BLK], shift, 1) for k in range(spans)]
            none = jnp.zeros_like(turned[0])
            keep = lane >= shift
            for k in range(spans + 1):
                here = turned[k] if k < spans else none
                before = turned[k - 1] if k else none
                to = pl.ds(aligned(start + k * BLK, BLK), BLK)
                total[c, pl.ds(top, PATCH + 8), to] += rows_to(jnp.where(keep, here, before), down)

    out_block = pl.ds(col_in, BLK)
    width = cols + BLK
    for c in range(2):
        grad[c] = total[c, RIM:last, BLK : BLK + cols]
        for half, wide in ((sx, own), (1 - sx, to_x)):
            wide[c, :, 0:cols] = pick_strips(total, c, RIM, rows, inner, half, h)
            wide[c, :, cols:width] = pick_strips(total, c, RIM, rows, out_block, half, h)
        for half, wide in ((sx, to_y), (1 - sx, to_d)):
            wide[c, :, 0:cols] = pick_strips(total, c, row_in, RIM, inner, half, h)
            wide[c, :, cols:width] = pick_strips(total, c, row_in, RIM, out_block, half, h)
        rim_x[c] = own[c, :, cols:width]
        probe_keep[c] = probe_total[sx, c]
        probe_send[c] = probe_total[1 - sx, c].astype(bf16)


def project_kernel(
    h, group, own, from_x, from_y, from_d, weight, to_core, keep, *outs_and_scratch
):
    outs, (rows_all, chunks) = outs_and_scratch[:-2], outs_and_scratch[-2:]
    sy, sx, me = lax.axis_index("sy"), lax.axis_index("sx"), lax.axis_index("ang")
    f32, bf16 = jnp.float32, jnp.bfloat16
    rows = own.shape[1]
    cols = own.shape[2] - BLK
    rims = from_y.shape[1]
    count = rows // h
    mine, other = pl.ds(aligned(sx * cols, BLK), cols), pl.ds(aligned((1 - sx) * cols, BLK), cols)
    rim_mine = pl.ds(aligned(sx * (cols - BLK) + (1 - sx) * cols, BLK), BLK)
    rim_other = pl.ds(aligned(sx * cols + (1 - sx) * (cols - BLK), BLK), BLK)
    at = pl.ds(aligned((1 - sy) * (rows - rims), rims), rims)
    edge = pl.ds(aligned(sx * (cols - BLK), BLK), BLK)
    for c in range(2):
        rows_all[c, :, mine] = own[c, :, 0:cols].astype(f32)
        rows_all[c, :, other] = from_x[c, :, 0:cols].astype(f32)
        rows_all[c, :, rim_mine] += own[c, :, cols:].astype(f32)
        rows_all[c, :, rim_other] += from_x[c, :, cols:].astype(f32)
        rows_all[c, at, mine] += from_y[c, :, 0:cols].astype(f32)
        rows_all[c, at, other] += from_d[c, :, 0:cols].astype(f32)
        rows_all[c, at, rim_mine] += from_y[c, :, cols:].astype(f32)
        rows_all[c, at, rim_other] += from_d[c, :, cols:].astype(f32)
        to_core[c] = from_d[c, :, 0:cols]
        to_core[c, :, edge] = (from_d[c, :, edge].astype(f32) + from_y[c, :, cols:].astype(f32)).astype(bf16)
        part = jnp.dot(rows_all[c].astype(bf16), weight[...], preferred_element_type=f32)
        for j in range(count):
            chunks[j, c * h : (c + 1) * h, :] = part[j * h : (j + 1) * h]
    keep[...] = chunks[me]
    for d in range(1, group):
        outs[d - 1][...] = chunks[me ^ d].astype(bf16)
    for d in range(group):
        for k in range(1, count // group):
            piece = chunks[me ^ d ^ (k * group)]
            ref = outs[group - 1 + d]
            ref[(k - 1) * 2 * h : k * 2 * h, :] = piece.astype(ref.dtype)


def fold_kernel(h, grad, from_x, rim_x, from_y, from_d, from_core, out):
    sy, sx = lax.axis_index("sy"), lax.axis_index("sx")
    f32 = jnp.float32
    rows, cols = grad.shape[1], grad.shape[2]
    edge = pl.ds(aligned((1 - sx) * (cols - BLK), BLK), BLK)
    row = aligned((1 - sy) * (rows - RIM), RIM)
    every = pl.ds(0, cols)
    for c in range(2):
        out[c] = grad[c]
        add_strips(out, c, 0, rows, edge, sx, h, from_x[c, :, cols:].astype(f32))
        add_strips(out, c, 0, rows, edge, 1 - sx, h, rim_x[c].astype(f32))
        add_strips(out, c, row, RIM, every, sx, h, from_y[c, :, 0:cols].astype(f32))
        add_strips(out, c, row, RIM, edge, sx, h, from_d[c, :, cols:].astype(f32))
        add_strips(out, c, row, RIM, every, 1 - sx, h, from_core[c].astype(f32))


def far_kernel(count, *refs):
    out = refs[-1]
    total = refs[0][...]
    for ref in refs[1:-1]:
        total += ref[...].astype(jnp.float32)
    total = total.astype(out.dtype)
    out[...] = total


def last_kernel(h, *refs):
    out = refs[-1]
    total = refs[0][...]
    for ref in refs[1:-1]:
        total += ref[...].astype(jnp.float32)
    for c in range(2):
        out[:, c, :] = total[c * h : (c + 1) * h]


def probe_kernel(scale, mine, other, out):
    sx = lax.axis_index("sx")
    out[sx] = mine[...].astype(jnp.float32) * scale
    out[1 - sx] = other[...].astype(jnp.float32) * scale


def body(objects, probe, data, positions, block_index, block_values):
    f32, bf16 = jnp.float32, jnp.bfloat16
    obj, measured, pos = objects[0], data[0, 0, 0], positions[0, 0, 0]
    rows, cols = obj.shape[1], obj.shape[2]
    modes, patches = probe.shape[0], measured.shape[0]
    n = lax.axis_size("ang")
    tiles = lax.axis_size("sy") * lax.axis_size("sx")
    h = rows // (n * lax.axis_size("sx"))
    strip_rows = rows // 2
    lines = block_values.shape[0]
    width = lines * BLK
    group = 1
    while group * group < n:
        group *= 2

    to_y, to_x, to_d = call(
        edge_kernel,
        (shape((2, RIM, cols)), shape((2, rows, BLK)), shape((2, RIM, BLK))),
        (obj,), [VMEM], moved=2 * MIB,
    )
    halo_y = lax.ppermute(to_y, "sy", SWAP)
    halo_d = lax.ppermute(to_d, ("sy", "sx"), CROSS)
    halo_x = lax.ppermute(to_x, "sx", SWAP)

    entries = block_index.size // n
    weight = call(
        partial(weight_kernel, entries),
        shape((width, width)),
        (block_index, block_values, jnp.asarray(ramp_table(width))),
        [SMEM, VMEM, VMEM],
        [pltpu.VMEM((width, width), f32), pltpu.SMEM((entries,), jnp.int32)],
        flops=2 * entries * width * BLK * BLK * 4, moved=8 * MIB,
    )

    wide = cols + BLK
    grad, own, to_x, rim_x, to_y, to_d, probe_keep, probe_send = call(
        partial(patch_kernel, h),
        (
            shape((2, rows, cols), f32),
            shape((2, strip_rows, wide)),
            shape((2, strip_rows, wide)),
            shape((2, strip_rows, BLK)),
            shape((2, RIM // 2, wide)),
            shape((2, RIM // 2, wide)),
            shape((2, PATCH, PATCH), f32),
            shape((2, PATCH, PATCH)),
        ),
        (pos, obj, halo_y, halo_x, halo_d, probe, measured, jnp.asarray(dft_blocks(PATCH))),
        [SMEM] + [VMEM] * 7,
        [
            pltpu.VMEM((2, rows + 2 * RIM + 8, cols + 2 * BLK), f32),
            pltpu.VMEM((2, rows + 2 * RIM + 8, cols + 2 * BLK), f32),
            pltpu.VMEM((2 * PATCH, patches * modes * PATCH), bf16),
            pltpu.VMEM((modes, 2, PATCH, PATCH), f32),
        ],
        limit=48, flops=patches * modes * 32 * PATCH**3, moved=8 * MIB,
    )

    from_x = lax.ppermute(to_x, "sx", SWAP)
    from_y = lax.ppermute(to_y, "sy", SWAP)
    from_d = lax.ppermute(to_d, ("sy", "sx"), CROSS)
    from_rim = lax.ppermute(rim_x, "sx", SWAP)
    probe_x = lax.ppermute(probe_send, "sx", SWAP)
    probe_mine = (probe_keep + probe_x.astype(f32)).astype(bf16)
    probe_y = lax.ppermute(probe_mine, "sy", SWAP)
    probe_mine = (probe_mine.astype(f32) + probe_y.astype(f32)).astype(bf16)
    probe_other = lax.ppermute(probe_mine, "sx", SWAP)

    far = n // group - 1
    outs = call(
        partial(project_kernel, h, group),
        (shape((2, RIM // 2, cols)), shape((2 * h, width), f32))
        + (shape((2 * h, width)),) * (group - 1)
        + (shape((far * 2 * h, width), f32),)
        + (shape((far * 2 * h, width)),) * (group - 1),
        (own, from_x, from_y, from_d, weight),
        [VMEM] * 5,
        [pltpu.VMEM((2, strip_rows, width), f32), pltpu.VMEM((n, 2 * h, width), f32)],
        flops=4 * strip_rows * width * width, moved=8 * MIB,
    )
    to_core, keep, near, away = outs[0], outs[1], outs[2 : 1 + group], outs[1 + group :]

    def swap(array, d):
        return lax.ppermute(array, "ang", [(i, i ^ d) for i in range(n)])

    got = [swap(away[d], d) for d in range(group - 1, 0, -1)]
    near_got = [swap(near[d - 1], d) for d in range(group - 1, 0, -1)]
    across = call(
        partial(far_kernel, far), shape((far * 2 * h, width)), [away[0]] + got, [VMEM] * group,
        moved=MIB,
    )
    across_got = [swap(across[(k - 1) * 2 * h : k * 2 * h], k * group) for k in range(1, far + 1)]
    from_core = lax.ppermute(to_core, "sx", SWAP)
    object_grad = call(
        partial(fold_kernel, h),
        shape((2, rows, cols), f32),
        (grad, from_x, from_rim, from_y, from_d, from_core),
        [VMEM] * 6, moved=6 * MIB,
    )
    probe_grad = call(
        partial(probe_kernel, 1.0 / math.sqrt(patches * tiles)),
        shape((modes, 2, PATCH, PATCH), f32),
        (probe_mine, probe_other),
        [VMEM] * 2, moved=2 * MIB,
    )
    vol = call(
        partial(last_kernel, h),
        shape((h, 2, width), f32),
        [keep] + near_got + across_got,
        [VMEM] * (group + far), moved=MIB,
    )
    return (object_grad[None], probe_grad[None], vol[None])


def solution(mesh):
    placed = (
        P("ang", None, "sy", "sx"),
        P(),
        P("ang", "sy", "sx", None, None, None),
        P("ang", "sy", "sx", None, None),
        P(),
        P(),
    )
    return jax.shard_map(
        body,
        mesh=mesh,
        in_specs=placed,
        out_specs=(
            P("ang", None, "sy", "sx"),
            P("ang", None, None, None, None),
            P("sy", ("ang", "sx"), None, None),
        ),
        check_vma=False,
    )
```

```python
from functools import partial
import math

import jax
import jax.numpy as jnp
import ml_dtypes
import numpy as np
from jax import lax
from jax.experimental import pallas as pl
from jax.experimental.pallas import tpu as pltpu
from jax.sharding import PartitionSpec as P

PATCH = 256
RIM = 64
BLK = 128
SWAP = [(0, 1), (1, 0)]
CROSS = [(0, 3), (3, 0), (1, 2), (2, 1)]
MIB = 1 << 20

VMEM = pl.BlockSpec(memory_space=pltpu.VMEM)
SMEM = pl.BlockSpec(memory_space=pltpu.SMEM)
ANY = pl.BlockSpec(memory_space=pl.ANY)
HBM = pl.BlockSpec(memory_space=pltpu.HBM)


def dft_blocks(length):
    ids = np.arange(length)
    phases = (ids[:, None] * ids[None, :] % length) * (2.0 * math.pi / length)
    factor = 1.0 / math.sqrt(length)
    re, im = np.cos(phases) * factor, -np.sin(phases) * factor
    forward = np.block([[re, -im], [im, re]])
    backward = np.block([[re, im], [-im, re]])
    return np.stack([forward, backward]).astype(np.float32).astype(ml_dtypes.bfloat16)


def ramp_strip(width):
    offsets = np.arange(2 * width - BLK)[None, :] - (width - BLK) - np.arange(BLK)[:, None]
    scaled = offsets.astype(np.float64) * math.pi
    values = np.where(offsets % 2 != 0, -1.0 / np.maximum(scaled * scaled, 1.0), 0.0)
    values = np.where(offsets == 0, 0.25, values)
    return values.astype(np.float32).astype(ml_dtypes.bfloat16)


def shape(dims, dtype=jnp.bfloat16):
    return jax.ShapeDtypeStruct(dims, dtype)


def call(kernel, outs, ins, specs, scratch=(), limit=16, flops=0, moved=0):
    ins = [
        pltpu.with_memory_space_constraint(x, pltpu.HBM) if spec is HBM else x
        for x, spec in zip(ins, specs, strict=True)
    ]
    return pl.pallas_call(
        kernel,
        out_shape=outs,
        in_specs=specs,
        out_specs=jax.tree.map(lambda _: VMEM, outs),
        scratch_shapes=list(scratch),
        compiler_params=pltpu.CompilerParams(vmem_limit_bytes=limit * MIB),
        cost_estimate=pl.CostEstimate(flops=flops, bytes_accessed=moved, transcendentals=0),
    )(*ins)


def aligned(value, step):
    return pl.multiple_of(value, step)


def edge_kernel(obj, to_y, to_x, to_d, sems):
    sy, sx = lax.axis_index("sy"), lax.axis_index("sx")
    rows, cols = obj.shape[1], obj.shape[2]
    r = pl.ds(aligned((1 - sy) * (rows - RIM), RIM), RIM)
    c = pl.ds(aligned((1 - sx) * (cols - BLK), BLK), BLK)
    copies = [
        pltpu.make_async_copy(obj.at[:, r, :], to_y, sems.at[0]),
        pltpu.make_async_copy(obj.at[:, r, c], to_d, sems.at[1]),
        pltpu.make_async_copy(obj.at[:, :, c], to_x, sems.at[2]),
    ]
    for copy in copies:
        copy.start()
    for copy in copies:
        copy.wait()


def gather_kernel(count, index, values, out, blocks, sums, index_here, found, slots, sems):
    me = lax.axis_index("ang")
    lines, per = index.shape
    first = pltpu.make_async_copy(index, index_here, sems.at[count])
    first.start()
    out[...] = jnp.zeros_like(out)
    for i in range(lines * lines):
        slots[i] = jnp.int32(count)
    first.wait()
    low, high = me * lines, (me + 1) * lines
    n = jnp.int32(0)
    for b in range(lines):
        for k in range(per):
            g = index_here[b, k]
            found[n] = jnp.int32(b * per + k)
            n = jnp.minimum(n + ((g >= low) & (g < high)).astype(jnp.int32), count)
    copies, places = [], []
    for i in range(count):
        e = found[i]
        b, k = lax.div(e, per), lax.rem(e, per)
        copies.append(pltpu.make_async_copy(values.at[b, k], blocks.at[i], sems.at[i]))
        copies[i].start()
        places.append((index_here[b, k] - low, b))
    for copy in copies:
        copy.wait()
    for i, (line, b) in enumerate(places):
        place = line * lines + b
        slot = jnp.minimum(slots[place], i)
        value = blocks[i].astype(jnp.float32)
        sums[slot] = jnp.where(slot < i, sums[slot] + value, value)
        slots[place] = slot
        row, col = pl.ds(aligned(line * BLK, BLK), BLK), pl.ds(aligned(b * BLK, BLK), BLK)
        out[row, col] = sums[slot].astype(out.dtype)


def weight_kernel(matrix, strip, *refs):
    steps = (len(refs) - 2) // 2
    sources, out, targets, sems = refs[:steps], refs[steps], refs[steps + 1 : -1], refs[-1]
    moves = [
        pltpu.make_async_copy(source, target, sems.at[i])
        for i, (source, target) in enumerate(zip(sources, targets, strict=True))
    ]
    for move in moves:
        move.start()
    width = out.shape[0]
    starts = range(width - BLK, -1, -BLK)
    ramp = jnp.concatenate([strip[:, start : start + width] for start in starts], axis=0)
    out[...] = jnp.dot(ramp, matrix[...], preferred_element_type=jnp.float32).astype(out.dtype)
    for move in moves:
        move.wait()


def strip_select(half, rows, h, dtype):
    i = lax.broadcasted_iota(jnp.int32, (rows // 2, rows), 0)
    j = lax.broadcasted_iota(jnp.int32, (rows // 2, rows), 1)
    return (j == i // h * 2 * h + half * h + i % h).astype(dtype)


def pick_strips(ref, c, row, rows, lanes, half, h):
    if h % 8 == 0:
        parts = [
            ref[c, pl.ds(aligned(row + q * 2 * h + half * h, 8), h), lanes]
            for q in range(rows // (2 * h))
        ]
        return jnp.concatenate(parts, axis=0).astype(jnp.bfloat16)
    whole = ref[c, pl.ds(aligned(row, 8), rows), lanes].astype(jnp.bfloat16)
    chosen = strip_select(half, rows, h, jnp.bfloat16)
    return jnp.dot(chosen, whole, preferred_element_type=jnp.float32).astype(jnp.bfloat16)


def add_strips(ref, c, row, rows, lanes, half, h, terms):
    if h % 8 == 0:
        for q in range(rows // (2 * h)):
            at = pl.ds(aligned(row + q * 2 * h + half * h, 8), h)
            ref[c, at, lanes] += terms[q * h : (q + 1) * h]
        return
    chosen = strip_select(half, rows, h, jnp.float32)
    at = pl.ds(aligned(row, 8), rows)
    ref[c, at, lanes] += lax.dot_general(
        chosen, terms, (((0,), (0,)), ((), ())), precision=lax.Precision.HIGHEST,
        preferred_element_type=jnp.float32,
    )


def rows_from(value, shift):
    rows, lanes = value.shape[0] - 8, value.shape[1]
    turned = pltpu.roll(value.reshape(rows // 8 + 1, 8, lanes), (8 - shift) % 8, 1)
    keep = lax.broadcasted_iota(jnp.int32, (rows // 8, 8, lanes), 1) < 8 - shift
    return jnp.where(keep, turned[:-1], turned[1:]).reshape(rows, lanes)


def rows_to(value, shift):
    rows, lanes = value.shape
    turned = pltpu.roll(value.reshape(rows // 8, 8, lanes), shift, 1)
    none = jnp.zeros((1, 8, lanes), value.dtype)
    keep = lax.broadcasted_iota(jnp.int32, (rows // 8 + 1, 8, lanes), 1) >= shift
    here = jnp.concatenate([turned, none], axis=0)
    before = jnp.concatenate([none, turned], axis=0)
    return jnp.where(keep, here, before).reshape(rows + 8, lanes)


def patch_kernel(
    h, pos, ahead, obj, from_y, from_x, from_d, probe, data, dft,
    grad, own, to_x, rim_x, to_y, to_d, probe_send,
    frame, total, stack, probe_total, spots, sem,
):
    fetch = pltpu.make_async_copy(pos, spots, sem)
    fetch.start()
    sy, sx = lax.axis_index("sy"), lax.axis_index("sx")
    rows, cols = obj.shape[1], obj.shape[2]
    modes = probe.shape[0]
    patches = data.shape[0]
    f32, bf16 = jnp.float32, jnp.bfloat16
    last = RIM + rows
    row_in = aligned((1 - sy) * last, RIM)
    row_out = aligned(sy * last, RIM)
    col_in = aligned((1 - sx) * (BLK + cols), BLK)
    col_out = aligned(sx * (BLK + cols), BLK)
    inner = pl.ds(BLK, cols)
    for c in range(2):
        frame[c, RIM:last, BLK : BLK + cols] = obj[c].astype(f32)
        frame[c, pl.ds(row_out, RIM), :] = jnp.zeros((RIM, frame.shape[2]), f32)
        frame[c, :, pl.ds(col_out, BLK)] = jnp.zeros((frame.shape[1], BLK), f32)
        frame[c, RIM:last, pl.ds(col_in, BLK)] = from_x[c].astype(f32)
        frame[c, pl.ds(row_in, RIM), inner] = from_y[c].astype(f32)
        frame[c, pl.ds(row_in, RIM), pl.ds(col_in, BLK)] = from_d[c].astype(f32)
    total[...] = jnp.zeros_like(total)
    lane = lax.broadcasted_iota(jnp.int32, (PATCH, BLK), 1)
    spans = PATCH // BLK
    fetch.wait()

    def place(p):
        u, v = spots[p, 0], spots[p, 1] + (BLK - RIM)
        start = aligned(v // BLK * BLK, BLK)
        top = aligned(u // 8 * 8, 8)
        return top, u - top, start, v - start

    def window(p):
        top, down, start, shift = place(p)
        out = []
        for c in range(2):
            cuts = [frame[c, pl.ds(top, PATCH + 8), pl.ds(aligned(start + k * BLK, BLK), BLK)] for k in range(spans + 1)]
            blocks = [pltpu.roll(rows_from(cut, down), (BLK - shift) % BLK, 1) for cut in cuts]
            keep = lane < BLK - shift
            out.append(
                jnp.concatenate([jnp.where(keep, blocks[k], blocks[k + 1]) for k in range(spans)], axis=1)
            )
        return out

    windows = [window(p) for p in range(patches)]
    for p in range(patches):
        o_re, o_im = windows[p]
        for m in range(modes):
            p_re, p_im = probe[m, 0], probe[m, 1]
            at = slice((p * modes + m) * PATCH, (p * modes + m + 1) * PATCH)
            stack[0:PATCH, at] = (p_re * o_re - p_im * o_im).astype(bf16)
            stack[PATCH:, at] = (p_re * o_im + p_im * o_re).astype(bf16)

    def transform(left, right, p):
        at = slice(p * modes * PATCH, (p + 1) * modes * PATCH)
        half = jnp.dot(dft[left], stack[:, at], preferred_element_type=f32).astype(bf16)
        out = []
        for m in range(modes):
            cut = slice(m * PATCH, (m + 1) * PATCH)
            wide = jnp.concatenate([half[:PATCH, cut], half[PATCH:, cut]], axis=1)
            out.append(jnp.dot(wide, dft[right], preferred_element_type=f32))
        return out

    for p in range(patches):
        far = transform(0, 1, p)
        misfit = sum(f[:, :PATCH] * f[:, :PATCH] + f[:, PATCH:] * f[:, PATCH:] for f in far)
        misfit = misfit - data[p].astype(f32)
        for m in range(modes):
            at = slice((p * modes + m) * PATCH, (p * modes + m + 1) * PATCH)
            stack[0:PATCH, at] = (misfit * far[m][:, :PATCH]).astype(bf16)
            stack[PATCH:, at] = (misfit * far[m][:, PATCH:]).astype(bf16)

    for p in range(patches):
        chi = transform(1, 0, p)
        o_re, o_im = windows[p]
        g_re = g_im = 0.0
        for m in range(modes):
            c_re, c_im = chi[m][:, :PATCH], chi[m][:, PATCH:]
            p_re, p_im = probe[m, 0], probe[m, 1]
            g_re += p_re * c_re + p_im * c_im
            g_im += p_re * c_im - p_im * c_re
            q_re, q_im = o_re * c_re + o_im * c_im, o_re * c_im - o_im * c_re
            if p == 0:
                probe_total[m, 0], probe_total[m, 1] = q_re, q_im
            else:
                probe_total[m, 0] += q_re
                probe_total[m, 1] += q_im
        top, down, start, shift = place(p)
        for c, g in enumerate((g_re, g_im)):
            turned = [pltpu.roll(g[:, k * BLK : (k + 1) * BLK], shift, 1) for k in range(spans)]
            none = jnp.zeros_like(turned[0])
            keep = lane >= shift
            for k in range(spans + 1):
                here = turned[k] if k < spans else none
                before = turned[k - 1] if k else none
                to = pl.ds(aligned(start + k * BLK, BLK), BLK)
                total[c, pl.ds(top, PATCH + 8), to] += rows_to(jnp.where(keep, here, before), down)

    out_block = pl.ds(col_in, BLK)
    width = cols + BLK
    for c in range(2):
        grad[c] = total[c, RIM:last, BLK : BLK + cols]
        for half, wide in ((sx, own), (1 - sx, to_x)):
            wide[c, :, 0:cols] = pick_strips(total, c, RIM, rows, inner, half, h)
            wide[c, :, cols:width] = pick_strips(total, c, RIM, rows, out_block, half, h)
        for half, wide in ((sx, to_y), (1 - sx, to_d)):
            wide[c, :, 0:cols] = pick_strips(total, c, row_in, RIM, inner, half, h)
            wide[c, :, cols:width] = pick_strips(total, c, row_in, RIM, out_block, half, h)
        rim_x[c] = own[c, :, cols:width]
    probe_send[...] = probe_total[...].astype(bf16)


def column_cuts(sx, cols):
    low, high = aligned(sx * cols, BLK), aligned((1 - sx) * cols, BLK)
    edge = cols - BLK
    mine = pl.ds(aligned(sx * edge + (1 - sx) * cols, BLK), BLK)
    other = pl.ds(aligned(sx * cols + (1 - sx) * edge, BLK), BLK)
    return pl.ds(low, cols), pl.ds(high, cols), mine, other


def project_kernel(h, own, from_x, weight, chunks, rows_all):
    sx = lax.axis_index("sx")
    f32, bf16 = jnp.float32, jnp.bfloat16
    cols = own.shape[2] - BLK
    count = own.shape[1] // h
    mine, other, rim_mine, rim_other = column_cuts(sx, cols)
    for c in range(2):
        rows_all[c, :, mine] = own[c, :, 0:cols].astype(f32)
        rows_all[c, :, other] = from_x[c, :, 0:cols].astype(f32)
        rows_all[c, :, rim_mine] += own[c, :, cols:].astype(f32)
        rows_all[c, :, rim_other] += from_x[c, :, cols:].astype(f32)
        rows = rows_all[c].astype(bf16)
        part = jnp.dot(rows, weight[...], preferred_element_type=f32)
        for j in range(count):
            chunks[j, c * h : (c + 1) * h, :] = part[j * h : (j + 1) * h]


def rim_kernel(
    h, group, from_y, from_d, weight, chunks, to_core, *outs_and_scratch
):
    outs, (rows_all, pieces) = outs_and_scratch[:-2], outs_and_scratch[-2:]
    sy, sx, me = lax.axis_index("sy"), lax.axis_index("sx"), lax.axis_index("ang")
    f32, bf16 = jnp.float32, jnp.bfloat16
    cols = from_y.shape[2] - BLK
    count = from_y.shape[1] // h
    mine, other, rim_mine, rim_other = column_cuts(sx, cols)
    edge = pl.ds(aligned(sx * (cols - BLK), BLK), BLK)
    for c in range(2):
        rows_all[c, :, mine] = from_y[c, :, 0:cols].astype(f32)
        rows_all[c, :, other] = from_d[c, :, 0:cols].astype(f32)
        rows_all[c, :, rim_mine] += from_y[c, :, cols:].astype(f32)
        rows_all[c, :, rim_other] += from_d[c, :, cols:].astype(f32)
        to_core[c] = from_d[c, :, 0:cols]
        to_core[c, :, edge] = (from_d[c, :, edge].astype(f32) + from_y[c, :, cols:].astype(f32)).astype(bf16)
    rows = rows_all[...].reshape(2 * count * h, 2 * cols).astype(bf16)
    part = jnp.dot(rows, weight[...], preferred_element_type=f32)
    for c in range(2):
        for q in range(count):
            row = (c * count + q) * h
            pieces[q, c * h : (c + 1) * h, :] = part[row : row + h]
    total = chunks.shape[0]
    base = (1 - sy) * (total - count)

    def piece(owner):
        rel = owner - base
        found = pieces[jnp.clip(rel, 0, count - 1)]
        return chunks[owner] + jnp.where((rel >= 0) & (rel < count), found, jnp.zeros_like(found))

    for d in range(group):
        outs[d][...] = piece(me ^ d).astype(outs[d].dtype)
        far = outs[group + d]
        for k in range(1, total // group):
            far[(k - 1) * 2 * h : k * 2 * h, :] = piece(me ^ d ^ (k * group)).astype(far.dtype)


def fold_kernel(h, grad, from_x, rim_x, from_y, from_d, from_core, out):
    sy, sx = lax.axis_index("sy"), lax.axis_index("sx")
    f32 = jnp.float32
    rows, cols = grad.shape[1], grad.shape[2]
    edge = pl.ds(aligned((1 - sx) * (cols - BLK), BLK), BLK)
    row = aligned((1 - sy) * (rows - RIM), RIM)
    every = pl.ds(0, cols)
    for c in range(2):
        out[c] = grad[c]
        add_strips(out, c, 0, rows, edge, sx, h, from_x[c, :, cols:].astype(f32))
        add_strips(out, c, 0, rows, edge, 1 - sx, h, rim_x[c].astype(f32))
        add_strips(out, c, row, RIM, every, sx, h, from_y[c, :, 0:cols].astype(f32))
        add_strips(out, c, row, RIM, edge, sx, h, from_d[c, :, cols:].astype(f32))
        add_strips(out, c, row, RIM, every, 1 - sx, h, from_core[c].astype(f32))


def far_kernel(*refs):
    out = refs[-1]
    total = refs[0][...]
    for ref in refs[1:-1]:
        total += ref[...].astype(jnp.float32)
    out[...] = total.astype(out.dtype)


def probe_sum_kernel(kept, received, after, out):
    out[...] = (kept[...].astype(jnp.float32) + received[...].astype(jnp.float32)).astype(out.dtype)


def last_kernel(h, *refs):
    out = refs[-1]
    total = refs[0][...]
    for ref in refs[1:-1]:
        total += ref[...].astype(jnp.float32)
    for c in range(2):
        out[:, c, :] = total[c * h : (c + 1) * h]


def probe_kernel(scale, mine, other, out):
    out[...] = (mine[...].astype(jnp.float32) + other[...].astype(jnp.float32)) * scale


def body(objects, probe, data, positions, block_index, block_values):
    f32, bf16 = jnp.float32, jnp.bfloat16
    obj, measured, pos = objects[0], data[0, 0, 0], positions[0, 0, 0]
    rows, cols = obj.shape[1], obj.shape[2]
    modes, patches = probe.shape[0], measured.shape[0]
    n = lax.axis_size("ang")
    tiles = lax.axis_size("sy") * lax.axis_size("sx")
    h = rows // (n * lax.axis_size("sx"))
    strip_rows = rows // 2
    lines = block_values.shape[0]
    width = lines * BLK
    group = 1
    while group * group < n:
        group *= 2

    to_y, to_x, to_d = call(
        edge_kernel,
        (shape((2, RIM, cols)), shape((2, rows, BLK)), shape((2, RIM, BLK))),
        (obj,), [HBM], [pltpu.SemaphoreType.DMA((3,))], moved=2 * MIB,
    )
    halo_y = lax.ppermute(to_y, "sy", SWAP)
    halo_d = lax.ppermute(to_d, ("sy", "sx"), CROSS)
    halo_x = lax.ppermute(to_x, "sx", SWAP)

    entries = block_index.size // n
    matrix = call(
        partial(gather_kernel, entries),
        shape((width, width)),
        (block_index, block_values),
        [HBM, HBM],
        [
            pltpu.VMEM((entries, BLK, BLK), bf16),
            pltpu.VMEM((entries, BLK, BLK), f32),
            pltpu.SMEM(block_index.shape, jnp.int32),
            pltpu.SMEM((entries + 1,), jnp.int32),
            pltpu.SMEM((lines * lines,), jnp.int32),
            pltpu.SemaphoreType.DMA((entries + 1,)),
        ],
        flops=MIB, moved=4 * MIB,
    )
    carried = (obj, probe, measured, jnp.asarray(dft_blocks(PATCH)))
    weight, obj, probe, measured, dft = call(
        weight_kernel,
        (shape((width, width)),) + tuple(shape(x.shape, x.dtype) for x in carried),
        (matrix, jnp.asarray(ramp_strip(width))) + carried,
        [VMEM, VMEM] + [HBM] * len(carried),
        [pltpu.SemaphoreType.DMA((len(carried),))],
        flops=2 * width**3, moved=6 * MIB,
    )

    wide = cols + BLK
    grad, own, to_x, rim_x, to_y, to_d, probe_here = call(
        partial(patch_kernel, h),
        (
            shape((2, rows, cols), f32),
            shape((2, strip_rows, wide)),
            shape((2, strip_rows, wide)),
            shape((2, strip_rows, BLK)),
            shape((2, RIM // 2, wide)),
            shape((2, RIM // 2, wide)),
            shape((modes, 2, PATCH, PATCH)),
        ),
        (pos, weight, obj, halo_y, halo_x, halo_d, probe, measured, dft),
        [HBM, ANY] + [VMEM] * 7,
        [
            pltpu.VMEM((2, rows + 2 * RIM + 8, cols + 2 * BLK), f32),
            pltpu.VMEM((2, rows + 2 * RIM + 8, cols + 2 * BLK), f32),
            pltpu.VMEM((2 * PATCH, patches * modes * PATCH), bf16),
            pltpu.VMEM((modes, 2, PATCH, PATCH), f32),
            pltpu.SMEM(pos.shape, jnp.int32),
            pltpu.SemaphoreType.DMA,
        ],
        limit=24, flops=patches * modes * 32 * PATCH**3, moved=8 * MIB,
    )

    from_x = lax.ppermute(to_x, "sx", SWAP)
    from_y = lax.ppermute(to_y, "sy", SWAP)
    from_d = lax.ppermute(to_d, ("sy", "sx"), CROSS)
    from_rim = lax.ppermute(rim_x, "sx", SWAP)
    probe_x = lax.ppermute(probe_here, "sx", SWAP)

    chunks = call(
        partial(project_kernel, h),
        shape((n, 2 * h, width), f32),
        (own, from_x, weight),
        [VMEM] * 3,
        [pltpu.VMEM((2, strip_rows, width), f32)],
        flops=4 * strip_rows * width * width, moved=8 * MIB,
    )
    far = n // group - 1
    outs = call(
        partial(rim_kernel, h, group),
        (shape((2, RIM // 2, cols)), shape((2 * h, width), f32))
        + (shape((2 * h, width)),) * (group - 1)
        + (shape((far * 2 * h, width), f32),)
        + (shape((far * 2 * h, width)),) * (group - 1),
        (from_y, from_d, weight, chunks),
        [VMEM] * 4,
        [pltpu.VMEM((2, RIM // 2, width), f32), pltpu.VMEM((RIM // (2 * h), 2 * h, width), f32)],
        flops=2 * RIM * width * width, moved=4 * MIB,
    )
    to_core, near, away = outs[0], outs[1 : 1 + group], outs[1 + group :]

    def swap(array, d):
        return lax.ppermute(array, "ang", [(i, i ^ d) for i in range(n)])

    got = [swap(away[d], d) for d in range(group - 1, 0, -1)]
    near_got = [swap(near[d], d) for d in range(group - 1, 0, -1)]
    across = call(
        far_kernel, shape((far * 2 * h, width)), [away[0]] + got, [VMEM] * group, moved=MIB,
    )
    across_got = [swap(across[(k - 1) * 2 * h : k * 2 * h], k * group) for k in range(1, far + 1)]

    probe_here = call(
        probe_sum_kernel, shape((modes, 2, PATCH, PATCH)), (probe_here, probe_x, to_core),
        [VMEM, VMEM, ANY], moved=MIB,
    )
    probe_y = lax.ppermute(probe_here, "sy", SWAP)
    from_core = lax.ppermute(to_core, "sx", SWAP)
    object_grad = call(
        partial(fold_kernel, h),
        shape((2, rows, cols), f32),
        (grad, from_x, from_rim, from_y, from_d, from_core),
        [VMEM] * 6, moved=6 * MIB,
    )
    probe_grad = call(
        partial(probe_kernel, 1.0 / math.sqrt(patches * tiles)),
        shape((modes, 2, PATCH, PATCH), f32),
        (probe_here, probe_y),
        [VMEM] * 2, moved=2 * MIB,
    )
    vol = call(
        partial(last_kernel, h),
        shape((h, 2, width), f32),
        [near[0]] + near_got + across_got,
        [VMEM] * (group + far), moved=MIB,
    )
    return (object_grad[None], probe_grad[None], vol[None])


def solution(mesh):
    placed = (
        P("ang", None, "sy", "sx"),
        P(),
        P("ang", "sy", "sx", None, None, None),
        P("ang", "sy", "sx", None, None),
        P(),
        P(),
    )
    return jax.shard_map(
        body,
        mesh=mesh,
        in_specs=placed,
        out_specs=(
            P("ang", None, "sy", "sx"),
            P("ang", None, None, None, None),
            P("sy", ("ang", "sx"), None, None),
        ),
        check_vma=False,
    )
```

```python
from functools import partial
import math

import jax
import jax.numpy as jnp
import ml_dtypes
import numpy as np
from jax import lax
from jax.experimental import pallas as pl
from jax.experimental.pallas import tpu as pltpu
from jax.sharding import PartitionSpec as P

PATCH = 256
RIM = 64
BLK = 128
SWAP = [(0, 1), (1, 0)]
CROSS = [(0, 3), (3, 0), (1, 2), (2, 1)]
MIB = 1 << 20

VMEM = pl.BlockSpec(memory_space=pltpu.VMEM)
SMEM = pl.BlockSpec(memory_space=pltpu.SMEM)
ANY = pl.BlockSpec(memory_space=pl.ANY)
HBM = pl.BlockSpec(memory_space=pltpu.HBM)


def dft_blocks(length):
    ids = np.arange(length)
    phases = (ids[:, None] * ids[None, :] % length) * (2.0 * math.pi / length)
    factor = 1.0 / math.sqrt(length)
    re, im = np.cos(phases) * factor, -np.sin(phases) * factor
    forward = np.block([[re, -im], [im, re]])
    backward = np.block([[re, im], [-im, re]])
    return np.stack([forward, backward]).astype(np.float32).astype(ml_dtypes.bfloat16)


def ramp_strip(width):
    offsets = np.arange(2 * width - BLK)[None, :] - (width - BLK) - np.arange(BLK)[:, None]
    scaled = offsets.astype(np.float64) * math.pi
    values = np.where(offsets % 2 != 0, -1.0 / np.maximum(scaled * scaled, 1.0), 0.0)
    values = np.where(offsets == 0, 0.25, values)
    return values.astype(np.float32).astype(ml_dtypes.bfloat16)


def shape(dims, dtype=jnp.bfloat16):
    return jax.ShapeDtypeStruct(dims, dtype)


def call(kernel, outs, ins, specs, scratch=(), limit=16, flops=0, moved=0):
    ins = [
        pltpu.with_memory_space_constraint(x, pltpu.HBM) if spec is HBM else x
        for x, spec in zip(ins, specs, strict=True)
    ]
    return pl.pallas_call(
        kernel,
        out_shape=outs,
        in_specs=specs,
        out_specs=jax.tree.map(lambda _: VMEM, outs),
        scratch_shapes=list(scratch),
        compiler_params=pltpu.CompilerParams(vmem_limit_bytes=limit * MIB),
        cost_estimate=pl.CostEstimate(flops=flops, bytes_accessed=moved, transcendentals=0),
    )(*ins)


def aligned(value, step):
    return pl.multiple_of(value, step)


def edge_kernel(obj, to_y, to_x, to_d, sems):
    sy, sx = lax.axis_index("sy"), lax.axis_index("sx")
    rows, cols = obj.shape[1], obj.shape[2]
    r = pl.ds(aligned((1 - sy) * (rows - RIM), RIM), RIM)
    c = pl.ds(aligned((1 - sx) * (cols - BLK), BLK), BLK)
    copies = [
        pltpu.make_async_copy(obj.at[:, r, :], to_y, sems.at[0]),
        pltpu.make_async_copy(obj.at[:, r, c], to_d, sems.at[1]),
        pltpu.make_async_copy(obj.at[:, :, c], to_x, sems.at[2]),
    ]
    for copy in copies:
        copy.start()
    for copy in copies:
        copy.wait()


def gather_kernel(count, index, values, out, blocks, sums, index_here, found, slots, sems):
    me = lax.axis_index("ang")
    lines, per = index.shape
    first = pltpu.make_async_copy(index, index_here, sems.at[count])
    first.start()
    out[...] = jnp.zeros_like(out)
    for i in range(lines * lines):
        slots[i] = jnp.int32(count)
    first.wait()
    low, high = me * lines, (me + 1) * lines
    n = jnp.int32(0)
    for b in range(lines):
        for k in range(per):
            g = index_here[b, k]
            found[n] = jnp.int32(b * per + k)
            n = jnp.minimum(n + ((g >= low) & (g < high)).astype(jnp.int32), count)
    copies, places = [], []
    for i in range(count):
        e = found[i]
        b, k = lax.div(e, per), lax.rem(e, per)
        copies.append(pltpu.make_async_copy(values.at[b, k], blocks.at[i], sems.at[i]))
        copies[i].start()
        places.append((index_here[b, k] - low, b))
    for copy in copies:
        copy.wait()
    for i, (line, b) in enumerate(places):
        place = line * lines + b
        slot = jnp.minimum(slots[place], i)
        value = blocks[i].astype(jnp.float32)
        sums[slot] = jnp.where(slot < i, sums[slot] + value, value)
        slots[place] = slot
        row, col = pl.ds(aligned(line * BLK, BLK), BLK), pl.ds(aligned(b * BLK, BLK), BLK)
        out[row, col] = sums[slot].astype(out.dtype)


def weight_kernel(matrix, strip, *refs):
    steps = (len(refs) - 2) // 2
    sources, out, targets, sems = refs[:steps], refs[steps], refs[steps + 1 : -1], refs[-1]
    moves = [
        pltpu.make_async_copy(source, target, sems.at[i])
        for i, (source, target) in enumerate(zip(sources, targets, strict=True))
    ]
    for move in moves:
        move.start()
    width = out.shape[0]
    starts = range(width - BLK, -1, -BLK)
    ramp = jnp.concatenate([strip[:, start : start + width] for start in starts], axis=0)
    out[...] = jnp.dot(ramp, matrix[...], preferred_element_type=jnp.float32).astype(out.dtype)
    for move in moves:
        move.wait()


def strip_select(half, rows, h, dtype):
    i = lax.broadcasted_iota(jnp.int32, (rows // 2, rows), 0)
    j = lax.broadcasted_iota(jnp.int32, (rows // 2, rows), 1)
    return (j == i // h * 2 * h + half * h + i % h).astype(dtype)


def pick_strips(ref, c, row, rows, lanes, half, h):
    if h % 8 == 0:
        parts = [
            ref[c, pl.ds(aligned(row + q * 2 * h + half * h, 8), h), lanes]
            for q in range(rows // (2 * h))
        ]
        return jnp.concatenate(parts, axis=0).astype(jnp.bfloat16)
    whole = ref[c, pl.ds(aligned(row, 8), rows), lanes].astype(jnp.bfloat16)
    chosen = strip_select(half, rows, h, jnp.bfloat16)
    return jnp.dot(chosen, whole, preferred_element_type=jnp.float32).astype(jnp.bfloat16)


def add_strips(ref, c, row, rows, lanes, half, h, terms):
    if h % 8 == 0:
        for q in range(rows // (2 * h)):
            at = pl.ds(aligned(row + q * 2 * h + half * h, 8), h)
            ref[c, at, lanes] += terms[q * h : (q + 1) * h]
        return
    chosen = strip_select(half, rows, h, jnp.float32)
    at = pl.ds(aligned(row, 8), rows)
    ref[c, at, lanes] += lax.dot_general(
        chosen, terms, (((0,), (0,)), ((), ())), precision=lax.Precision.HIGHEST,
        preferred_element_type=jnp.float32,
    )


def rows_from(value, shift):
    rows, lanes = value.shape[0] - 8, value.shape[1]
    turned = pltpu.roll(value.reshape(rows // 8 + 1, 8, lanes), (8 - shift) % 8, 1)
    keep = lax.broadcasted_iota(jnp.int32, (rows // 8, 8, lanes), 1) < 8 - shift
    return jnp.where(keep, turned[:-1], turned[1:]).reshape(rows, lanes)


def rows_to(value, shift):
    rows, lanes = value.shape
    turned = pltpu.roll(value.reshape(rows // 8, 8, lanes), shift, 1)
    none = jnp.zeros((1, 8, lanes), value.dtype)
    keep = lax.broadcasted_iota(jnp.int32, (rows // 8 + 1, 8, lanes), 1) >= shift
    here = jnp.concatenate([turned, none], axis=0)
    before = jnp.concatenate([none, turned], axis=0)
    return jnp.where(keep, here, before).reshape(rows + 8, lanes)


def patch_kernel(
    h, pos, ahead, obj, from_y, from_x, from_d, probe, data, dft,
    grad, own, to_x, to_y, to_d, probe_here,
    frame, total, stack, probe_total, spots, sem,
):
    fetch = pltpu.make_async_copy(pos, spots, sem)
    fetch.start()
    sy, sx = lax.axis_index("sy"), lax.axis_index("sx")
    rows, cols = obj.shape[1], obj.shape[2]
    modes = probe.shape[0]
    patches = data.shape[0]
    f32, bf16 = jnp.float32, jnp.bfloat16
    last = RIM + rows
    row_in = aligned((1 - sy) * last, RIM)
    row_out = aligned(sy * last, RIM)
    col_in = aligned((1 - sx) * (BLK + cols), BLK)
    col_out = aligned(sx * (BLK + cols), BLK)
    inner = pl.ds(BLK, cols)
    for c in range(2):
        frame[c, RIM:last, BLK : BLK + cols] = obj[c].astype(f32)
        frame[c, pl.ds(row_out, RIM), :] = jnp.zeros((RIM, frame.shape[2]), f32)
        frame[c, :, pl.ds(col_out, BLK)] = jnp.zeros((frame.shape[1], BLK), f32)
        frame[c, RIM:last, pl.ds(col_in, BLK)] = from_x[c].astype(f32)
        frame[c, pl.ds(row_in, RIM), inner] = from_y[c].astype(f32)
        frame[c, pl.ds(row_in, RIM), pl.ds(col_in, BLK)] = from_d[c].astype(f32)
    total[...] = jnp.zeros_like(total)
    lane = lax.broadcasted_iota(jnp.int32, (PATCH, BLK), 1)
    spans = PATCH // BLK
    fetch.wait()

    def place(p):
        u, v = spots[p, 0], spots[p, 1] + (BLK - RIM)
        start = aligned(v // BLK * BLK, BLK)
        top = aligned(u // 8 * 8, 8)
        return top, u - top, start, v - start

    def window(p):
        top, down, start, shift = place(p)
        out = []
        for c in range(2):
            cuts = [frame[c, pl.ds(top, PATCH + 8), pl.ds(aligned(start + k * BLK, BLK), BLK)] for k in range(spans + 1)]
            blocks = [pltpu.roll(rows_from(cut, down), (BLK - shift) % BLK, 1) for cut in cuts]
            keep = lane < BLK - shift
            out.append(
                jnp.concatenate([jnp.where(keep, blocks[k], blocks[k + 1]) for k in range(spans)], axis=1)
            )
        return out

    windows = [window(p) for p in range(patches)]
    for p in range(patches):
        o_re, o_im = windows[p]
        for m in range(modes):
            p_re, p_im = probe[m, 0], probe[m, 1]
            at = slice((p * modes + m) * PATCH, (p * modes + m + 1) * PATCH)
            stack[0:PATCH, at] = (p_re * o_re - p_im * o_im).astype(bf16)
            stack[PATCH:, at] = (p_re * o_im + p_im * o_re).astype(bf16)

    def transform(left, right, p):
        at = slice(p * modes * PATCH, (p + 1) * modes * PATCH)
        half = jnp.dot(dft[left], stack[:, at], preferred_element_type=f32).astype(bf16)
        out = []
        for m in range(modes):
            cut = slice(m * PATCH, (m + 1) * PATCH)
            wide = jnp.concatenate([half[:PATCH, cut], half[PATCH:, cut]], axis=1)
            out.append(jnp.dot(wide, dft[right], preferred_element_type=f32))
        return out

    for p in range(patches):
        far = transform(0, 1, p)
        misfit = sum(f[:, :PATCH] * f[:, :PATCH] + f[:, PATCH:] * f[:, PATCH:] for f in far)
        misfit = misfit - data[p].astype(f32)
        for m in range(modes):
            at = slice((p * modes + m) * PATCH, (p * modes + m + 1) * PATCH)
            stack[0:PATCH, at] = (misfit * far[m][:, :PATCH]).astype(bf16)
            stack[PATCH:, at] = (misfit * far[m][:, PATCH:]).astype(bf16)

    for p in range(patches):
        chi = transform(1, 0, p)
        o_re, o_im = windows[p]
        g_re = g_im = 0.0
        for m in range(modes):
            c_re, c_im = chi[m][:, :PATCH], chi[m][:, PATCH:]
            p_re, p_im = probe[m, 0], probe[m, 1]
            g_re += p_re * c_re + p_im * c_im
            g_im += p_re * c_im - p_im * c_re
            q_re, q_im = o_re * c_re + o_im * c_im, o_re * c_im - o_im * c_re
            if p == 0:
                probe_total[m, 0], probe_total[m, 1] = q_re, q_im
            else:
                probe_total[m, 0] += q_re
                probe_total[m, 1] += q_im
        top, down, start, shift = place(p)
        for c, g in enumerate((g_re, g_im)):
            turned = [pltpu.roll(g[:, k * BLK : (k + 1) * BLK], shift, 1) for k in range(spans)]
            none = jnp.zeros_like(turned[0])
            keep = lane >= shift
            for k in range(spans + 1):
                here = turned[k] if k < spans else none
                before = turned[k - 1] if k else none
                to = pl.ds(aligned(start + k * BLK, BLK), BLK)
                total[c, pl.ds(top, PATCH + 8), to] += rows_to(jnp.where(keep, here, before), down)

    out_block = pl.ds(col_in, BLK)
    width = cols + BLK
    for c in range(2):
        grad[c] = total[c, RIM:last, BLK : BLK + cols]
        for half, wide in ((sx, own), (1 - sx, to_x)):
            wide[c, :, 0:cols] = pick_strips(total, c, RIM, rows, inner, half, h)
            wide[c, :, cols:width] = pick_strips(total, c, RIM, rows, out_block, half, h)
        for half, wide in ((sx, to_y), (1 - sx, to_d)):
            wide[c, :, 0:cols] = pick_strips(total, c, row_in, RIM, inner, half, h)
            wide[c, :, cols:width] = pick_strips(total, c, row_in, RIM, out_block, half, h)
        to_x[c, :, width : width + BLK] = own[c, :, cols:width]
    probe_here[...] = probe_total[...].astype(bf16)


def column_cuts(sx, cols):
    low, high = aligned(sx * cols, BLK), aligned((1 - sx) * cols, BLK)
    edge = cols - BLK
    mine = pl.ds(aligned(sx * edge + (1 - sx) * cols, BLK), BLK)
    other = pl.ds(aligned(sx * cols + (1 - sx) * edge, BLK), BLK)
    return pl.ds(low, cols), pl.ds(high, cols), mine, other


def at_home(group, total, count):
    return lax.axis_index("ang") // group == (1 - lax.axis_index("sy")) * (total - count) // group


def owner_of(first, group, d, k):
    me = lax.axis_index("ang")
    return jnp.where(first, me ^ d ^ (k * group), me ^ d)


def project_kernel(h, group, rims, own, from_x, weight, chunks, *outs_and_scratch):
    outs, rows_all = outs_and_scratch[:-1], outs_and_scratch[-1]
    sx = lax.axis_index("sx")
    f32, bf16 = jnp.float32, jnp.bfloat16
    cols = own.shape[2] - BLK
    count = own.shape[1] // h
    mine, other, rim_mine, rim_other = column_cuts(sx, cols)
    for c in range(2):
        rows_all[c, :, mine] = own[c, :, 0:cols].astype(f32)
        rows_all[c, :, other] = from_x[c, :, 0:cols].astype(f32)
        rows_all[c, :, rim_mine] += own[c, :, cols:].astype(f32)
        rows_all[c, :, rim_other] += from_x[c, :, cols : cols + BLK].astype(f32)
        rows = rows_all[c].astype(bf16)
        part = jnp.dot(rows, weight[...], preferred_element_type=f32)
        for j in range(count):
            chunks[j, c * h : (c + 1) * h, :] = part[j * h : (j + 1) * h]
    home = at_home(group, count, rims)
    for d, ref in enumerate(outs):
        for k in range(1, count // group):
            part = chunks[owner_of(home, group, d, k)]
            ref[(k - 1) * 2 * h : k * 2 * h, :] = part.astype(ref.dtype)


def rim_kernel(
    h, group, after, from_y, from_d, weight, chunks, *outs_and_scratch
):
    outs, (rows_all, pieces) = outs_and_scratch[:-2], outs_and_scratch[-2:]
    sy, sx = lax.axis_index("sy"), lax.axis_index("sx")
    f32, bf16 = jnp.float32, jnp.bfloat16
    cols = from_y.shape[2] - BLK
    count = from_y.shape[1] // h
    mine, other, rim_mine, rim_other = column_cuts(sx, cols)
    for c in range(2):
        rows_all[c, :, mine] = from_y[c, :, 0:cols].astype(f32)
        rows_all[c, :, other] = from_d[c, :, 0:cols].astype(f32)
        rows_all[c, :, rim_mine] += from_y[c, :, cols:].astype(f32)
        rows_all[c, :, rim_other] += from_d[c, :, cols:].astype(f32)
    rows = rows_all[...].reshape(2 * count * h, 2 * cols).astype(bf16)
    part = jnp.dot(rows, weight[...], preferred_element_type=f32)
    for c in range(2):
        for q in range(count):
            row = (c * count + q) * h
            pieces[q, c * h : (c + 1) * h, :] = part[row : row + h]
    total = chunks.shape[0]
    base = (1 - sy) * (total - count)
    away = jnp.logical_not(at_home(group, total, count))
    for d, ref in enumerate(outs):
        for k in range(1, total // group):
            owner = owner_of(away, group, d, k)
            rel = owner - base
            found = pieces[jnp.clip(rel, 0, count - 1)]
            part = chunks[owner] + jnp.where((rel >= 0) & (rel < count), found, jnp.zeros_like(found))
            ref[(k - 1) * 2 * h : k * 2 * h, :] = part.astype(ref.dtype)


def fold_kernel(h, grad, from_x, from_y, from_d, from_core, out):
    sy, sx = lax.axis_index("sy"), lax.axis_index("sx")
    f32 = jnp.float32
    rows, cols = grad.shape[1], grad.shape[2]
    edge = pl.ds(aligned((1 - sx) * (cols - BLK), BLK), BLK)
    row = aligned((1 - sy) * (rows - RIM), RIM)
    every = pl.ds(0, cols)
    for c in range(2):
        out[c] = grad[c]
        add_strips(out, c, 0, rows, edge, sx, h, from_x[c, :, cols : cols + BLK].astype(f32))
        add_strips(out, c, 0, rows, edge, 1 - sx, h, from_x[c, :, cols + BLK : cols + 2 * BLK].astype(f32))
        add_strips(out, c, row, RIM, every, sx, h, from_y[c, :, 0:cols].astype(f32))
        add_strips(out, c, row, RIM, edge, sx, h, from_d[c, :, cols:].astype(f32))
        add_strips(out, c, row, RIM, every, 1 - sx, h, from_core[c].astype(f32))


def add(refs):
    total = refs[0][...]
    for ref in refs[1:]:
        total += ref[...].astype(jnp.float32)
    return total


def early_kernel(*refs):
    refs[-1][...] = add(refs[:-1])


def group_kernel(group, total, rims, from_y, from_d, early, *refs):
    late, (across, near, to_core) = refs[:group], refs[group:]
    first, second = early[...], add(late)
    home = at_home(group, total, rims)
    across[...] = jnp.where(home, first, second).astype(across.dtype)
    near[...] = jnp.where(home, second, first)[: near.shape[0]]
    cols = to_core.shape[2]
    edge = pl.ds(aligned(lax.axis_index("sx") * (cols - BLK), BLK), BLK)
    to_core[...] = from_d[:, :, 0:cols]
    at_edge = from_d[:, :, edge].astype(jnp.float32) + from_y[:, :, cols:].astype(jnp.float32)
    to_core[:, :, edge] = at_edge.astype(to_core.dtype)


def probe_sum_kernel(after, kept, received, out):
    out[...] = (kept[...].astype(jnp.float32) + received[...].astype(jnp.float32)).astype(out.dtype)


def last_kernel(h, after, *refs):
    out = refs[-1]
    total = refs[0][...]
    for ref in refs[1:-1]:
        total += ref[...].astype(jnp.float32)
    for c in range(2):
        out[:, c, :] = total[c * h : (c + 1) * h]


def probe_kernel(scale, mine, other, out):
    out[...] = (mine[...].astype(jnp.float32) + other[...].astype(jnp.float32)) * scale


def body(objects, probe, data, positions, block_index, block_values):
    f32, bf16 = jnp.float32, jnp.bfloat16
    obj, measured, pos = objects[0], data[0, 0, 0], positions[0, 0, 0]
    rows, cols = obj.shape[1], obj.shape[2]
    modes, patches = probe.shape[0], measured.shape[0]
    n = lax.axis_size("ang")
    tiles = lax.axis_size("sy") * lax.axis_size("sx")
    h = rows // (n * lax.axis_size("sx"))
    strip_rows = rows // 2
    lines = block_values.shape[0]
    width = lines * BLK
    group = 1
    while group * group < n:
        group *= 2

    to_y, to_x, to_d = call(
        edge_kernel,
        (shape((2, RIM, cols)), shape((2, rows, BLK)), shape((2, RIM, BLK))),
        (obj,), [HBM], [pltpu.SemaphoreType.DMA((3,))], moved=2 * MIB,
    )
    halo_y = lax.ppermute(to_y, "sy", SWAP)
    halo_d = lax.ppermute(to_d, ("sy", "sx"), CROSS)
    halo_x = lax.ppermute(to_x, "sx", SWAP)

    entries = block_index.size // n
    matrix = call(
        partial(gather_kernel, entries),
        shape((width, width)),
        (block_index, block_values),
        [HBM, HBM],
        [
            pltpu.VMEM((entries, BLK, BLK), bf16),
            pltpu.VMEM((entries, BLK, BLK), f32),
            pltpu.SMEM(block_index.shape, jnp.int32),
            pltpu.SMEM((entries + 1,), jnp.int32),
            pltpu.SMEM((lines * lines,), jnp.int32),
            pltpu.SemaphoreType.DMA((entries + 1,)),
        ],
        flops=MIB, moved=4 * MIB,
    )
    carried = (obj, probe, measured, jnp.asarray(dft_blocks(PATCH)))
    weight, obj, probe, measured, dft = call(
        weight_kernel,
        (shape((width, width)),) + tuple(shape(x.shape, x.dtype) for x in carried),
        (matrix, jnp.asarray(ramp_strip(width))) + carried,
        [VMEM, VMEM] + [HBM] * len(carried),
        [pltpu.SemaphoreType.DMA((len(carried),))],
        flops=2 * width**3, moved=6 * MIB,
    )

    wide = cols + BLK
    grad, own, to_x, to_y, to_d, probe_here = call(
        partial(patch_kernel, h),
        (
            shape((2, rows, cols), f32),
            shape((2, strip_rows, wide)),
            shape((2, strip_rows, wide + BLK)),
            shape((2, RIM // 2, wide)),
            shape((2, RIM // 2, wide)),
            shape((modes, 2, PATCH, PATCH)),
        ),
        (pos, weight, obj, halo_y, halo_x, halo_d, probe, measured, dft),
        [HBM, ANY] + [VMEM] * 7,
        [
            pltpu.VMEM((2, rows + 2 * RIM + 8, cols + 2 * BLK), f32),
            pltpu.VMEM((2, rows + 2 * RIM + 8, cols + 2 * BLK), f32),
            pltpu.VMEM((2 * PATCH, patches * modes * PATCH), bf16),
            pltpu.VMEM((modes, 2, PATCH, PATCH), f32),
            pltpu.SMEM(pos.shape, jnp.int32),
            pltpu.SemaphoreType.DMA,
        ],
        limit=24, flops=patches * modes * 32 * PATCH**3, moved=8 * MIB,
    )

    from_x = lax.ppermute(to_x, "sx", SWAP)
    probe_x = lax.ppermute(probe_here, "sx", SWAP)
    from_y = lax.ppermute(to_y, "sy", SWAP)
    from_d = lax.ppermute(to_d, ("sy", "sx"), CROSS)

    far = n // group - 1
    rims = RIM // (2 * h)
    parts = (shape((far * 2 * h, width), f32),) + (shape((far * 2 * h, width)),) * (group - 1)
    chunks, *early = call(
        partial(project_kernel, h, group, rims),
        (shape((n, 2 * h, width), f32),) + parts,
        (own, from_x, weight),
        [VMEM] * 3,
        [pltpu.VMEM((2, strip_rows, width), f32)],
        flops=4 * strip_rows * width * width, moved=8 * MIB,
    )
    probe_here = call(
        probe_sum_kernel, shape((modes, 2, PATCH, PATCH)), (chunks, probe_here, probe_x),
        [ANY, VMEM, VMEM], moved=MIB,
    )
    late = call(
        partial(rim_kernel, h, group),
        parts,
        (probe_here, from_y, from_d, weight, chunks),
        [ANY] + [VMEM] * 4,
        [pltpu.VMEM((2, RIM // 2, width), f32), pltpu.VMEM((rims, 2 * h, width), f32)],
        flops=12 * width**3, moved=4 * MIB,
    )

    def swap(array, d):
        return lax.ppermute(array, "ang", [(i, i ^ d) for i in range(n)])

    order = range(1, group)
    late_here, late = late[0], list(late)
    early[1:] = [swap(early[d], d) for d in order]
    late[1:] = [swap(late[d], d) for d in order]
    early = call(early_kernel, parts[0], early, [VMEM] * group, flops=16 * width**3 // 4, moved=MIB)
    across, near, to_core = call(
        partial(group_kernel, group, n, rims),
        (shape((far * 2 * h, width)), shape((2 * h, width), f32), shape((2, RIM // 2, cols))),
        [from_y, from_d, early] + late, [VMEM] * (3 + group), moved=MIB,
    )
    across_got = [swap(across[(k - 1) * 2 * h : k * 2 * h], k * group) for k in range(1, far + 1)]

    probe_y = lax.ppermute(probe_here, "sy", SWAP)
    from_core = lax.ppermute(to_core, "sx", SWAP)
    object_grad = call(
        partial(fold_kernel, h),
        shape((2, rows, cols), f32),
        (grad, from_x, from_y, from_d, from_core),
        [VMEM] * 5, moved=6 * MIB,
    )
    probe_grad = call(
        partial(probe_kernel, 1.0 / math.sqrt(patches * tiles)),
        shape((modes, 2, PATCH, PATCH), f32),
        (probe_here, probe_y),
        [VMEM] * 2, moved=2 * MIB,
    )
    vol = call(
        partial(last_kernel, h),
        shape((h, 2, width), f32),
        [probe_grad, near] + across_got,
        [HBM] + [VMEM] * (1 + far), moved=MIB,
    )
    return (object_grad[None], probe_grad[None], vol[None])


def solution(mesh):
    placed = (
        P("ang", None, "sy", "sx"),
        P(),
        P("ang", "sy", "sx", None, None, None),
        P("ang", "sy", "sx", None, None),
        P(),
        P(),
    )
    return jax.shard_map(
        body,
        mesh=mesh,
        in_specs=placed,
        out_specs=(
            P("ang", None, "sy", "sx"),
            P("ang", None, None, None, None),
            P("sy", ("ang", "sx"), None, None),
        ),
        check_vma=False,
    )
```

```python
from functools import partial
import math

import jax
import jax.numpy as jnp
import ml_dtypes
import numpy as np
from jax import lax
from jax.experimental import pallas as pl
from jax.experimental.pallas import tpu as pltpu
from jax.sharding import PartitionSpec as P

PATCH = 256
RIM = 64
BLK = 128
SWAP = [(0, 1), (1, 0)]
CROSS = [(0, 3), (3, 0), (1, 2), (2, 1)]
MIB = 1 << 20

VMEM = pl.BlockSpec(memory_space=pltpu.VMEM)
SMEM = pl.BlockSpec(memory_space=pltpu.SMEM)
ANY = pl.BlockSpec(memory_space=pl.ANY)
HBM = pl.BlockSpec(memory_space=pltpu.HBM)


def dft_blocks(length):
    ids = np.arange(length)
    phases = (ids[:, None] * ids[None, :] % length) * (2.0 * math.pi / length)
    factor = 1.0 / math.sqrt(length)
    re, im = np.cos(phases) * factor, -np.sin(phases) * factor
    forward = np.block([[re, -im], [im, re]])
    backward = np.block([[re, im], [-im, re]])
    return np.stack([forward, backward]).astype(np.float32).astype(ml_dtypes.bfloat16)


def ramp_strip(width):
    offsets = np.arange(2 * width - BLK)[None, :] - (width - BLK) - np.arange(BLK)[:, None]
    scaled = offsets.astype(np.float64) * math.pi
    values = np.where(offsets % 2 != 0, -1.0 / np.maximum(scaled * scaled, 1.0), 0.0)
    values = np.where(offsets == 0, 0.25, values)
    return values.astype(np.float32).astype(ml_dtypes.bfloat16)


def shape(dims, dtype=jnp.bfloat16):
    return jax.ShapeDtypeStruct(dims, dtype)


def call(kernel, outs, ins, specs, scratch=(), limit=16, flops=0, moved=0):
    ins = [
        pltpu.with_memory_space_constraint(x, pltpu.HBM) if spec is HBM else x
        for x, spec in zip(ins, specs, strict=True)
    ]
    return pl.pallas_call(
        kernel,
        out_shape=outs,
        in_specs=specs,
        out_specs=jax.tree.map(lambda _: VMEM, outs),
        scratch_shapes=list(scratch),
        compiler_params=pltpu.CompilerParams(vmem_limit_bytes=limit * MIB),
        cost_estimate=pl.CostEstimate(flops=flops, bytes_accessed=moved, transcendentals=0),
    )(*ins)


def aligned(value, step):
    return pl.multiple_of(value, step)


def edge_kernel(obj, to_y, to_x, to_d, sems):
    sy, sx = lax.axis_index("sy"), lax.axis_index("sx")
    rows, cols = obj.shape[1], obj.shape[2]
    r = pl.ds(aligned((1 - sy) * (rows - RIM), RIM), RIM)
    c = pl.ds(aligned((1 - sx) * (cols - BLK), BLK), BLK)
    copies = [
        pltpu.make_async_copy(obj.at[:, r, :], to_y, sems.at[0]),
        pltpu.make_async_copy(obj.at[:, r, c], to_d, sems.at[1]),
        pltpu.make_async_copy(obj.at[:, :, c], to_x, sems.at[2]),
    ]
    for copy in copies:
        copy.start()
    for copy in copies:
        copy.wait()


def gather_kernel(count, index, values, out, blocks, sums, index_here, found, slots, sems):
    me = lax.axis_index("ang")
    lines, per = index.shape
    first = pltpu.make_async_copy(index, index_here, sems.at[count])
    first.start()
    out[...] = jnp.zeros_like(out)
    for i in range(lines * lines):
        slots[i] = jnp.int32(count)
    first.wait()
    low, high = me * lines, (me + 1) * lines
    n = jnp.int32(0)
    for b in range(lines):
        for k in range(per):
            g = index_here[b, k]
            found[n] = jnp.int32(b * per + k)
            n = jnp.minimum(n + ((g >= low) & (g < high)).astype(jnp.int32), count)
    copies, places = [], []
    for i in range(count):
        e = found[i]
        b, k = lax.div(e, per), lax.rem(e, per)
        copies.append(pltpu.make_async_copy(values.at[b, k], blocks.at[i], sems.at[i]))
        copies[i].start()
        places.append((index_here[b, k] - low, b))
    for copy in copies:
        copy.wait()
    for i, (line, b) in enumerate(places):
        place = line * lines + b
        slot = jnp.minimum(slots[place], i)
        value = blocks[i].astype(jnp.float32)
        sums[slot] = jnp.where(slot < i, sums[slot] + value, value)
        slots[place] = slot
        row, col = pl.ds(aligned(line * BLK, BLK), BLK), pl.ds(aligned(b * BLK, BLK), BLK)
        out[row, col] = sums[slot].astype(out.dtype)


def weight_kernel(matrix, strip, *refs):
    steps = (len(refs) - 2) // 2
    sources, out, targets, sems = refs[:steps], refs[steps], refs[steps + 1 : -1], refs[-1]
    moves = [
        pltpu.make_async_copy(source, target, sems.at[i])
        for i, (source, target) in enumerate(zip(sources, targets, strict=True))
    ]
    for move in moves:
        move.start()
    width = out.shape[0]
    starts = range(width - BLK, -1, -BLK)
    ramp = jnp.concatenate([strip[:, start : start + width] for start in starts], axis=0)
    out[...] = jnp.dot(ramp, matrix[...], preferred_element_type=jnp.float32).astype(out.dtype)
    for move in moves:
        move.wait()


def strip_select(half, rows, h, dtype):
    i = lax.broadcasted_iota(jnp.int32, (rows // 2, rows), 0)
    j = lax.broadcasted_iota(jnp.int32, (rows // 2, rows), 1)
    return (j == i // h * 2 * h + half * h + i % h).astype(dtype)


def pick_strips(ref, c, row, rows, lanes, half, h):
    if h % 8 == 0:
        parts = [
            ref[c, pl.ds(aligned(row + q * 2 * h + half * h, 8), h), lanes]
            for q in range(rows // (2 * h))
        ]
        return jnp.concatenate(parts, axis=0).astype(jnp.bfloat16)
    whole = ref[c, pl.ds(aligned(row, 8), rows), lanes].astype(jnp.bfloat16)
    chosen = strip_select(half, rows, h, jnp.bfloat16)
    return jnp.dot(chosen, whole, preferred_element_type=jnp.float32).astype(jnp.bfloat16)


def add_strips(ref, c, row, rows, lanes, half, h, terms):
    if h % 8 == 0:
        for q in range(rows // (2 * h)):
            at = pl.ds(aligned(row + q * 2 * h + half * h, 8), h)
            ref[c, at, lanes] += terms[q * h : (q + 1) * h]
        return
    chosen = strip_select(half, rows, h, jnp.float32)
    at = pl.ds(aligned(row, 8), rows)
    ref[c, at, lanes] += lax.dot_general(
        chosen, terms, (((0,), (0,)), ((), ())), precision=lax.Precision.HIGHEST,
        preferred_element_type=jnp.float32,
    )


def rows_from(value, shift):
    rows, lanes = value.shape[0] - 8, value.shape[1]
    turned = pltpu.roll(value.reshape(rows // 8 + 1, 8, lanes), (8 - shift) % 8, 1)
    keep = lax.broadcasted_iota(jnp.int32, (rows // 8, 8, lanes), 1) < 8 - shift
    return jnp.where(keep, turned[:-1], turned[1:]).reshape(rows, lanes)


def rows_to(value, shift):
    rows, lanes = value.shape
    turned = pltpu.roll(value.reshape(rows // 8, 8, lanes), shift, 1)
    none = jnp.zeros((1, 8, lanes), value.dtype)
    keep = lax.broadcasted_iota(jnp.int32, (rows // 8 + 1, 8, lanes), 1) >= shift
    here = jnp.concatenate([turned, none], axis=0)
    before = jnp.concatenate([none, turned], axis=0)
    return jnp.where(keep, here, before).reshape(rows + 8, lanes)


def patch_kernel(
    h, pos, ahead, obj, from_y, from_x, from_d, probe, data, dft,
    grad, own, to_x, to_y, to_d, probe_here,
    frame, total, stack, probe_total, spots, sem,
):
    fetch = pltpu.make_async_copy(pos, spots, sem)
    fetch.start()
    sy, sx = lax.axis_index("sy"), lax.axis_index("sx")
    rows, cols = obj.shape[1], obj.shape[2]
    modes = probe.shape[0]
    patches = data.shape[0]
    f32, bf16 = jnp.float32, jnp.bfloat16
    last = RIM + rows
    row_in = aligned((1 - sy) * last, RIM)
    row_out = aligned(sy * last, RIM)
    col_in = aligned((1 - sx) * (BLK + cols), BLK)
    col_out = aligned(sx * (BLK + cols), BLK)
    inner = pl.ds(BLK, cols)
    for c in range(2):
        frame[c, RIM:last, BLK : BLK + cols] = obj[c].astype(f32)
        frame[c, pl.ds(row_out, RIM), :] = jnp.zeros((RIM, frame.shape[2]), f32)
        frame[c, :, pl.ds(col_out, BLK)] = jnp.zeros((frame.shape[1], BLK), f32)
        frame[c, RIM:last, pl.ds(col_in, BLK)] = from_x[c].astype(f32)
        frame[c, pl.ds(row_in, RIM), inner] = from_y[c].astype(f32)
        frame[c, pl.ds(row_in, RIM), pl.ds(col_in, BLK)] = from_d[c].astype(f32)
    total[...] = jnp.zeros_like(total)
    lane = lax.broadcasted_iota(jnp.int32, (PATCH, BLK), 1)
    spans = PATCH // BLK
    fetch.wait()

    def place(p):
        u, v = spots[p, 0], spots[p, 1] + (BLK - RIM)
        start = aligned(v // BLK * BLK, BLK)
        top = aligned(u // 8 * 8, 8)
        return top, u - top, start, v - start

    def window(p):
        top, down, start, shift = place(p)
        out = []
        for c in range(2):
            cuts = [frame[c, pl.ds(top, PATCH + 8), pl.ds(aligned(start + k * BLK, BLK), BLK)] for k in range(spans + 1)]
            blocks = [pltpu.roll(rows_from(cut, down), (BLK - shift) % BLK, 1) for cut in cuts]
            keep = lane < BLK - shift
            out.append(
                jnp.concatenate([jnp.where(keep, blocks[k], blocks[k + 1]) for k in range(spans)], axis=1)
            )
        return out

    windows = [window(p) for p in range(patches)]
    for p in range(patches):
        o_re, o_im = windows[p]
        for m in range(modes):
            p_re, p_im = probe[m, 0], probe[m, 1]
            at = slice((p * modes + m) * PATCH, (p * modes + m + 1) * PATCH)
            stack[0:PATCH, at] = (p_re * o_re - p_im * o_im).astype(bf16)
            stack[PATCH:, at] = (p_re * o_im + p_im * o_re).astype(bf16)

    def transform(left, right, p):
        at = slice(p * modes * PATCH, (p + 1) * modes * PATCH)
        half = jnp.dot(dft[left], stack[:, at], preferred_element_type=f32).astype(bf16)
        out = []
        for m in range(modes):
            cut = slice(m * PATCH, (m + 1) * PATCH)
            wide = jnp.concatenate([half[:PATCH, cut], half[PATCH:, cut]], axis=1)
            out.append(jnp.dot(wide, dft[right], preferred_element_type=f32))
        return out

    for p in range(patches):
        far = transform(0, 1, p)
        misfit = sum(f[:, :PATCH] * f[:, :PATCH] + f[:, PATCH:] * f[:, PATCH:] for f in far)
        misfit = misfit - data[p].astype(f32)
        for m in range(modes):
            at = slice((p * modes + m) * PATCH, (p * modes + m + 1) * PATCH)
            stack[0:PATCH, at] = (misfit * far[m][:, :PATCH]).astype(bf16)
            stack[PATCH:, at] = (misfit * far[m][:, PATCH:]).astype(bf16)

    for p in range(patches):
        chi = transform(1, 0, p)
        o_re, o_im = windows[p]
        g_re = g_im = 0.0
        for m in range(modes):
            c_re, c_im = chi[m][:, :PATCH], chi[m][:, PATCH:]
            p_re, p_im = probe[m, 0], probe[m, 1]
            g_re += p_re * c_re + p_im * c_im
            g_im += p_re * c_im - p_im * c_re
            q_re, q_im = o_re * c_re + o_im * c_im, o_re * c_im - o_im * c_re
            if p == 0:
                probe_total[m, 0], probe_total[m, 1] = q_re, q_im
            else:
                probe_total[m, 0] += q_re
                probe_total[m, 1] += q_im
        top, down, start, shift = place(p)
        for c, g in enumerate((g_re, g_im)):
            turned = [pltpu.roll(g[:, k * BLK : (k + 1) * BLK], shift, 1) for k in range(spans)]
            none = jnp.zeros_like(turned[0])
            keep = lane >= shift
            for k in range(spans + 1):
                here = turned[k] if k < spans else none
                before = turned[k - 1] if k else none
                to = pl.ds(aligned(start + k * BLK, BLK), BLK)
                total[c, pl.ds(top, PATCH + 8), to] += rows_to(jnp.where(keep, here, before), down)

    out_block = pl.ds(col_in, BLK)
    width = cols + BLK
    for c in range(2):
        grad[c] = total[c, RIM:last, BLK : BLK + cols]
        for half, wide in ((sx, own), (1 - sx, to_x)):
            wide[c, :, 0:cols] = pick_strips(total, c, RIM, rows, inner, half, h)
            wide[c, :, cols:width] = pick_strips(total, c, RIM, rows, out_block, half, h)
        for half, wide in ((sx, to_y), (1 - sx, to_d)):
            wide[c, :, 0:cols] = pick_strips(total, c, row_in, RIM, inner, half, h)
            wide[c, :, cols:width] = pick_strips(total, c, row_in, RIM, out_block, half, h)
        to_x[c, :, width : width + BLK] = own[c, :, cols:width]
    probe_here[...] = probe_total[...].astype(bf16)


def column_cuts(sx, cols):
    low, high = aligned(sx * cols, BLK), aligned((1 - sx) * cols, BLK)
    edge = cols - BLK
    mine = pl.ds(aligned(sx * edge + (1 - sx) * cols, BLK), BLK)
    other = pl.ds(aligned(sx * cols + (1 - sx) * edge, BLK), BLK)
    return pl.ds(low, cols), pl.ds(high, cols), mine, other


def at_home(group, total, count):
    return lax.axis_index("ang") // group == (1 - lax.axis_index("sy")) * (total - count) // group


def owner_of(first, group, d, k):
    me = lax.axis_index("ang")
    return jnp.where(first, me ^ d ^ (k * group), me ^ d)


def project_kernel(h, group, rims, half, after, own, from_x, weight, chunks, *outs_and_scratch):
    outs, rows_all = outs_and_scratch[:-1], outs_and_scratch[-1]
    sx, me = lax.axis_index("sx"), lax.axis_index("ang")
    f32, bf16 = jnp.float32, jnp.bfloat16
    cols = own.shape[2] - BLK
    total = own.shape[1] // h
    home = at_home(group, total, rims)
    rows = rows_all.shape[1]
    served = 0
    if half is not None:
        served = (me // group) ^ jnp.where(home, 1 - half, half)
    at = pl.ds(aligned(served * rows, rows), rows)
    mine, other, rim_mine, rim_other = column_cuts(sx, cols)
    for c in range(2):
        rows_all[c, :, mine] = own[c, at, 0:cols].astype(f32)
        rows_all[c, :, other] = from_x[c, at, 0:cols].astype(f32)
        rows_all[c, :, rim_mine] += own[c, at, cols:].astype(f32)
        rows_all[c, :, rim_other] += from_x[c, at, cols : cols + BLK].astype(f32)
    stacked = rows_all[...].reshape(2 * rows, 2 * cols).astype(bf16)
    part = jnp.dot(stacked, weight[...], preferred_element_type=f32)
    for c in range(2):
        for j in range(rows // h):
            row = c * rows + j * h
            chunks[j, c * h : (c + 1) * h, :] = part[row : row + h]
    for d, ref in enumerate(outs):
        for k in range(1, total // group):
            owner = owner_of(home, group, d, k) - served * (rows // h)
            ref[(k - 1) * 2 * h : k * 2 * h, :] = chunks[owner].astype(ref.dtype)


def rim_kernel(
    h, group, total, after, from_y, from_d, weight, chunks, *outs_and_scratch
):
    outs, (rows_all, pieces) = outs_and_scratch[:-2], outs_and_scratch[-2:]
    sy, sx = lax.axis_index("sy"), lax.axis_index("sx")
    f32, bf16 = jnp.float32, jnp.bfloat16
    cols = from_y.shape[2] - BLK
    count = from_y.shape[1] // h
    mine, other, rim_mine, rim_other = column_cuts(sx, cols)
    for c in range(2):
        rows_all[c, :, mine] = from_y[c, :, 0:cols].astype(f32)
        rows_all[c, :, other] = from_d[c, :, 0:cols].astype(f32)
        rows_all[c, :, rim_mine] += from_y[c, :, cols:].astype(f32)
        rows_all[c, :, rim_other] += from_d[c, :, cols:].astype(f32)
    rows = rows_all[...].reshape(2 * count * h, 2 * cols).astype(bf16)
    part = jnp.dot(rows, weight[...], preferred_element_type=f32)
    for c in range(2):
        for q in range(count):
            row = (c * count + q) * h
            pieces[q, c * h : (c + 1) * h, :] = part[row : row + h]
    held = chunks.shape[0]
    base = (1 - sy) * (total - count)
    away = jnp.logical_not(at_home(group, total, count))
    for d, ref in enumerate(outs):
        for k in range(1, total // group):
            owner = owner_of(away, group, d, k)
            rel = owner - base
            found = pieces[jnp.clip(rel, 0, count - 1)]
            part = chunks[owner % held] + jnp.where((rel >= 0) & (rel < count), found, jnp.zeros_like(found))
            ref[(k - 1) * 2 * h : k * 2 * h, :] = part.astype(ref.dtype)


def fold_kernel(h, grad, from_x, from_y, from_d, from_core, out):
    sy, sx = lax.axis_index("sy"), lax.axis_index("sx")
    f32 = jnp.float32
    rows, cols = grad.shape[1], grad.shape[2]
    edge = pl.ds(aligned((1 - sx) * (cols - BLK), BLK), BLK)
    row = aligned((1 - sy) * (rows - RIM), RIM)
    every = pl.ds(0, cols)
    for c in range(2):
        out[c] = grad[c]
        add_strips(out, c, 0, rows, edge, sx, h, from_x[c, :, cols : cols + BLK].astype(f32))
        add_strips(out, c, 0, rows, edge, 1 - sx, h, from_x[c, :, cols + BLK : cols + 2 * BLK].astype(f32))
        add_strips(out, c, row, RIM, every, sx, h, from_y[c, :, 0:cols].astype(f32))
        add_strips(out, c, row, RIM, edge, sx, h, from_d[c, :, cols:].astype(f32))
        add_strips(out, c, row, RIM, every, 1 - sx, h, from_core[c].astype(f32))


def add(refs):
    total = refs[0][...]
    for ref in refs[1:]:
        total += ref[...].astype(jnp.float32)
    return total


def early_kernel(*refs):
    refs[-1][...] = add(refs[:-1])


def group_kernel(group, total, rims, from_y, from_d, early, *refs):
    late, (across, near, to_core) = refs[:group], refs[group:]
    first, second = early[...], add(late)
    home = at_home(group, total, rims)
    across[...] = jnp.where(home, first, second).astype(across.dtype)
    near[...] = jnp.where(home, second, first)[: near.shape[0]]
    cols = to_core.shape[2]
    edge = pl.ds(aligned(lax.axis_index("sx") * (cols - BLK), BLK), BLK)
    to_core[...] = from_d[:, :, 0:cols]
    at_edge = from_d[:, :, edge].astype(jnp.float32) + from_y[:, :, cols:].astype(jnp.float32)
    to_core[:, :, edge] = at_edge.astype(to_core.dtype)


def probe_sum_kernel(after, kept, received, out):
    out[...] = (kept[...].astype(jnp.float32) + received[...].astype(jnp.float32)).astype(out.dtype)


def last_kernel(h, after, *refs):
    out = refs[-1]
    total = refs[0][...]
    for ref in refs[1:-1]:
        total += ref[...].astype(jnp.float32)
    for c in range(2):
        out[:, c, :] = total[c * h : (c + 1) * h]


def probe_kernel(scale, mine, other, out):
    out[...] = (mine[...].astype(jnp.float32) + other[...].astype(jnp.float32)) * scale


def body(objects, probe, data, positions, block_index, block_values):
    f32, bf16 = jnp.float32, jnp.bfloat16
    obj, measured, pos = objects[0], data[0, 0, 0], positions[0, 0, 0]
    rows, cols = obj.shape[1], obj.shape[2]
    modes, patches = probe.shape[0], measured.shape[0]
    n = lax.axis_size("ang")
    tiles = lax.axis_size("sy") * lax.axis_size("sx")
    h = rows // (n * lax.axis_size("sx"))
    strip_rows = rows // 2
    lines = block_values.shape[0]
    width = lines * BLK
    group = 1
    while group * group < n:
        group *= 2

    to_y, to_x, to_d = call(
        edge_kernel,
        (shape((2, RIM, cols)), shape((2, rows, BLK)), shape((2, RIM, BLK))),
        (obj,), [HBM], [pltpu.SemaphoreType.DMA((3,))], moved=2 * MIB,
    )
    halo_y = lax.ppermute(to_y, "sy", SWAP)
    halo_d = lax.ppermute(to_d, ("sy", "sx"), CROSS)
    halo_x = lax.ppermute(to_x, "sx", SWAP)

    entries = block_index.size // n
    matrix = call(
        partial(gather_kernel, entries),
        shape((width, width)),
        (block_index, block_values),
        [HBM, HBM],
        [
            pltpu.VMEM((entries, BLK, BLK), bf16),
            pltpu.VMEM((entries, BLK, BLK), f32),
            pltpu.SMEM(block_index.shape, jnp.int32),
            pltpu.SMEM((entries + 1,), jnp.int32),
            pltpu.SMEM((lines * lines,), jnp.int32),
            pltpu.SemaphoreType.DMA((entries + 1,)),
        ],
        flops=MIB, moved=4 * MIB,
    )
    carried = (obj, probe, measured, jnp.asarray(dft_blocks(PATCH)))
    weight, obj, probe, measured, dft = call(
        weight_kernel,
        (shape((width, width)),) + tuple(shape(x.shape, x.dtype) for x in carried),
        (matrix, jnp.asarray(ramp_strip(width))) + carried,
        [VMEM, VMEM] + [HBM] * len(carried),
        [pltpu.SemaphoreType.DMA((len(carried),))],
        flops=2 * width**3, moved=6 * MIB,
    )

    wide = cols + BLK
    grad, own, to_x, to_y, to_d, probe_here = call(
        partial(patch_kernel, h),
        (
            shape((2, rows, cols), f32),
            shape((2, strip_rows, wide)),
            shape((2, strip_rows, wide + BLK)),
            shape((2, RIM // 2, wide)),
            shape((2, RIM // 2, wide)),
            shape((modes, 2, PATCH, PATCH)),
        ),
        (pos, weight, obj, halo_y, halo_x, halo_d, probe, measured, dft),
        [HBM, ANY] + [VMEM] * 7,
        [
            pltpu.VMEM((2, rows + 2 * RIM + 8, cols + 2 * BLK), f32),
            pltpu.VMEM((2, rows + 2 * RIM + 8, cols + 2 * BLK), f32),
            pltpu.VMEM((2 * PATCH, patches * modes * PATCH), bf16),
            pltpu.VMEM((modes, 2, PATCH, PATCH), f32),
            pltpu.SMEM(pos.shape, jnp.int32),
            pltpu.SemaphoreType.DMA,
        ],
        limit=24, flops=patches * modes * 32 * PATCH**3, moved=8 * MIB,
    )

    from_x = lax.ppermute(to_x, "sx", SWAP)
    probe_x = lax.ppermute(probe_here, "sx", SWAP)
    from_y = lax.ppermute(to_y, "sy", SWAP)
    from_d = lax.ppermute(to_d, ("sy", "sx"), CROSS)

    far = n // group - 1
    rims = RIM // (2 * h)
    parts = (shape((far * 2 * h, width), f32),) + (shape((far * 2 * h, width)),) * (group - 1)
    split = far == 1

    def project(half, after, sent):
        rows = strip_rows // 2 if split else strip_rows
        return call(
            partial(project_kernel, h, group, rims, half),
            (shape((rows // h, 2 * h, width), f32),) + sent,
            (after, own, from_x, weight),
            [ANY] + [VMEM] * 3,
            [pltpu.VMEM((2, rows, width), f32)],
            flops=4 * rows * width * width, moved=8 * MIB,
        )

    chunks, *early = project(0 if split else None, weight, parts)
    if split:
        (chunks,) = project(1, chunks, ())
    probe_here = call(
        probe_sum_kernel, shape((modes, 2, PATCH, PATCH)), (early[0], probe_here, probe_x),
        [ANY, VMEM, VMEM], moved=MIB,
    )
    late = call(
        partial(rim_kernel, h, group, n),
        parts,
        (probe_here, from_y, from_d, weight, chunks),
        [ANY] + [VMEM] * 4,
        [pltpu.VMEM((2, RIM // 2, width), f32), pltpu.VMEM((rims, 2 * h, width), f32)],
        flops=12 * width**3, moved=4 * MIB,
    )

    def swap(array, d):
        return lax.ppermute(array, "ang", [(i, i ^ d) for i in range(n)])

    order = range(1, group)
    late_here, late = late[0], list(late)
    early[1:] = [swap(early[d], d) for d in order]
    late[1:] = [swap(late[d], d) for d in order]
    early = call(early_kernel, parts[0], early, [VMEM] * group, flops=16 * width**3 // 4, moved=MIB)
    across, near, to_core = call(
        partial(group_kernel, group, n, rims),
        (shape((far * 2 * h, width)), shape((2 * h, width), f32), shape((2, RIM // 2, cols))),
        [from_y, from_d, early] + late, [VMEM] * (3 + group), moved=MIB,
    )
    across_got = [swap(across[(k - 1) * 2 * h : k * 2 * h], k * group) for k in range(1, far + 1)]

    probe_y = lax.ppermute(probe_here, "sy", SWAP)
    from_core = lax.ppermute(to_core, "sx", SWAP)
    object_grad = call(
        partial(fold_kernel, h),
        shape((2, rows, cols), f32),
        (grad, from_x, from_y, from_d, from_core),
        [VMEM] * 5, moved=6 * MIB,
    )
    probe_grad = call(
        partial(probe_kernel, 1.0 / math.sqrt(patches * tiles)),
        shape((modes, 2, PATCH, PATCH), f32),
        (probe_here, probe_y),
        [VMEM] * 2, moved=2 * MIB,
    )
    vol = call(
        partial(last_kernel, h),
        shape((h, 2, width), f32),
        [probe_grad, near] + across_got,
        [HBM] + [VMEM] * (1 + far), moved=MIB,
    )
    return (object_grad[None], probe_grad[None], vol[None])


def solution(mesh):
    placed = (
        P("ang", None, "sy", "sx"),
        P(),
        P("ang", "sy", "sx", None, None, None),
        P("ang", "sy", "sx", None, None),
        P(),
        P(),
    )
    return jax.shard_map(
        body,
        mesh=mesh,
        in_specs=placed,
        out_specs=(
            P("ang", None, "sy", "sx"),
            P("ang", None, None, None, None),
            P("sy", ("ang", "sx"), None, None),
        ),
        check_vma=False,
    )
```

```python
from functools import partial
import math

import jax
import jax.numpy as jnp
import ml_dtypes
import numpy as np
from jax import lax
from jax.experimental import pallas as pl
from jax.experimental.pallas import tpu as pltpu
from jax.sharding import PartitionSpec as P

PATCH = 256
RIM = 64
BLK = 128
SWAP = [(0, 1), (1, 0)]
CROSS = [(0, 3), (3, 0), (1, 2), (2, 1)]
MIB = 1 << 20

VMEM = pl.BlockSpec(memory_space=pltpu.VMEM)
SMEM = pl.BlockSpec(memory_space=pltpu.SMEM)
ANY = pl.BlockSpec(memory_space=pl.ANY)
HBM = pl.BlockSpec(memory_space=pltpu.HBM)


def dft_blocks(length):
    ids = np.arange(length)
    phases = (ids[:, None] * ids[None, :] % length) * (2.0 * math.pi / length)
    factor = 1.0 / math.sqrt(length)
    re, im = np.cos(phases) * factor, -np.sin(phases) * factor
    forward = np.block([[re, -im], [im, re]])
    backward = np.block([[re, im], [-im, re]])
    return np.stack([forward, backward]).astype(np.float32).astype(ml_dtypes.bfloat16)


def ramp_strip(width):
    offsets = np.arange(2 * width - BLK)[None, :] - (width - BLK) - np.arange(BLK)[:, None]
    scaled = offsets.astype(np.float64) * math.pi
    values = np.where(offsets % 2 != 0, -1.0 / np.maximum(scaled * scaled, 1.0), 0.0)
    values = np.where(offsets == 0, 0.25, values)
    return values.astype(np.float32).astype(ml_dtypes.bfloat16)


def shape(dims, dtype=jnp.bfloat16):
    return jax.ShapeDtypeStruct(dims, dtype)


def call(kernel, outs, ins, specs, scratch=(), limit=16, flops=0, moved=0):
    ins = [
        pltpu.with_memory_space_constraint(x, pltpu.HBM) if spec is HBM else x
        for x, spec in zip(ins, specs, strict=True)
    ]
    return pl.pallas_call(
        kernel,
        out_shape=outs,
        in_specs=specs,
        out_specs=jax.tree.map(lambda _: VMEM, outs),
        scratch_shapes=list(scratch),
        compiler_params=pltpu.CompilerParams(vmem_limit_bytes=limit * MIB),
        cost_estimate=pl.CostEstimate(flops=flops, bytes_accessed=moved, transcendentals=0),
    )(*ins)


def aligned(value, step):
    return pl.multiple_of(value, step)


def edge_kernel(obj, to_y, to_x, to_d, sems):
    sy, sx = lax.axis_index("sy"), lax.axis_index("sx")
    rows, cols = obj.shape[1], obj.shape[2]
    r = pl.ds(aligned((1 - sy) * (rows - RIM), RIM), RIM)
    c = pl.ds(aligned((1 - sx) * (cols - BLK), BLK), BLK)
    copies = [
        pltpu.make_async_copy(obj.at[:, r, :], to_y, sems.at[0]),
        pltpu.make_async_copy(obj.at[:, r, c], to_d, sems.at[1]),
        pltpu.make_async_copy(obj.at[:, :, c], to_x, sems.at[2]),
    ]
    for copy in copies:
        copy.start()
    for copy in copies:
        copy.wait()


def gather_kernel(count, index, values, out, blocks, sums, index_here, found, slots, sems):
    me = lax.axis_index("ang")
    lines, per = index.shape
    first = pltpu.make_async_copy(index, index_here, sems.at[count])
    first.start()
    out[...] = jnp.zeros_like(out)
    for i in range(lines * lines):
        slots[i] = jnp.int32(count)
    first.wait()
    low, high = me * lines, (me + 1) * lines
    n = jnp.int32(0)
    for b in range(lines):
        for k in range(per):
            g = index_here[b, k]
            found[n] = jnp.int32(b * per + k)
            n = jnp.minimum(n + ((g >= low) & (g < high)).astype(jnp.int32), count)
    copies, places = [], []
    for i in range(count):
        e = found[i]
        b, k = lax.div(e, per), lax.rem(e, per)
        copies.append(pltpu.make_async_copy(values.at[b, k], blocks.at[i], sems.at[i]))
        copies[i].start()
        places.append((index_here[b, k] - low, b))
    for copy in copies:
        copy.wait()
    for i, (line, b) in enumerate(places):
        place = line * lines + b
        slot = jnp.minimum(slots[place], i)
        value = blocks[i].astype(jnp.float32)
        sums[slot] = jnp.where(slot < i, sums[slot] + value, value)
        slots[place] = slot
        row, col = pl.ds(aligned(line * BLK, BLK), BLK), pl.ds(aligned(b * BLK, BLK), BLK)
        out[row, col] = sums[slot].astype(out.dtype)


def weight_kernel(matrix, strip, *refs):
    steps = (len(refs) - 2) // 2
    sources, out, targets, sems = refs[:steps], refs[steps], refs[steps + 1 : -1], refs[-1]
    moves = [
        pltpu.make_async_copy(source, target, sems.at[i])
        for i, (source, target) in enumerate(zip(sources, targets, strict=True))
    ]
    for move in moves:
        move.start()
    width = out.shape[0]
    starts = range(width - BLK, -1, -BLK)
    ramp = jnp.concatenate([strip[:, start : start + width] for start in starts], axis=0)
    out[...] = jnp.dot(ramp, matrix[...], preferred_element_type=jnp.float32).astype(out.dtype)
    for move in moves:
        move.wait()


def strip_select(half, rows, h, dtype):
    i = lax.broadcasted_iota(jnp.int32, (rows // 2, rows), 0)
    j = lax.broadcasted_iota(jnp.int32, (rows // 2, rows), 1)
    return (j == i // h * 2 * h + half * h + i % h).astype(dtype)


def pick_strips(ref, c, row, rows, lanes, half, h):
    if h % 8 == 0:
        parts = [
            ref[c, pl.ds(aligned(row + q * 2 * h + half * h, 8), h), lanes]
            for q in range(rows // (2 * h))
        ]
        return jnp.concatenate(parts, axis=0).astype(jnp.bfloat16)
    whole = ref[c, pl.ds(aligned(row, 8), rows), lanes].astype(jnp.bfloat16)
    chosen = strip_select(half, rows, h, jnp.bfloat16)
    return jnp.dot(chosen, whole, preferred_element_type=jnp.float32).astype(jnp.bfloat16)


def add_strips(ref, c, row, rows, lanes, half, h, terms):
    if h % 8 == 0:
        for q in range(rows // (2 * h)):
            at = pl.ds(aligned(row + q * 2 * h + half * h, 8), h)
            ref[c, at, lanes] += terms[q * h : (q + 1) * h]
        return
    chosen = strip_select(half, rows, h, jnp.float32)
    at = pl.ds(aligned(row, 8), rows)
    ref[c, at, lanes] += lax.dot_general(
        chosen, terms, (((0,), (0,)), ((), ())), precision=lax.Precision.HIGHEST,
        preferred_element_type=jnp.float32,
    )


def rows_from(value, shift):
    rows, lanes = value.shape[0] - 8, value.shape[1]
    turned = pltpu.roll(value.reshape(rows // 8 + 1, 8, lanes), (8 - shift) % 8, 1)
    keep = lax.broadcasted_iota(jnp.int32, (rows // 8, 8, lanes), 1) < 8 - shift
    return jnp.where(keep, turned[:-1], turned[1:]).reshape(rows, lanes)


def rows_to(value, shift):
    rows, lanes = value.shape
    turned = pltpu.roll(value.reshape(rows // 8, 8, lanes), shift, 1)
    none = jnp.zeros((1, 8, lanes), value.dtype)
    keep = lax.broadcasted_iota(jnp.int32, (rows // 8 + 1, 8, lanes), 1) >= shift
    here = jnp.concatenate([turned, none], axis=0)
    before = jnp.concatenate([none, turned], axis=0)
    return jnp.where(keep, here, before).reshape(rows + 8, lanes)


def patch_kernel(
    h, pos, ahead, obj, from_y, from_x, from_d, probe, data, dft,
    total, own, to_x, to_y, to_d, probe_here,
    frame, stack, probe_total, spots, sem,
):
    fetch = pltpu.make_async_copy(pos, spots, sem)
    fetch.start()
    sy, sx = lax.axis_index("sy"), lax.axis_index("sx")
    rows, cols = obj.shape[1], obj.shape[2]
    modes = probe.shape[0]
    patches = data.shape[0]
    f32, bf16 = jnp.float32, jnp.bfloat16
    last = RIM + rows
    row_in = aligned((1 - sy) * last, RIM)
    row_out = aligned(sy * last, RIM)
    col_in = aligned((1 - sx) * (BLK + cols), BLK)
    col_out = aligned(sx * (BLK + cols), BLK)
    inner = pl.ds(BLK, cols)
    for c in range(2):
        frame[c, RIM:last, BLK : BLK + cols] = obj[c].astype(f32)
        frame[c, pl.ds(row_out, RIM), :] = jnp.zeros((RIM, frame.shape[2]), f32)
        frame[c, :, pl.ds(col_out, BLK)] = jnp.zeros((frame.shape[1], BLK), f32)
        frame[c, RIM:last, pl.ds(col_in, BLK)] = from_x[c].astype(f32)
        frame[c, pl.ds(row_in, RIM), inner] = from_y[c].astype(f32)
        frame[c, pl.ds(row_in, RIM), pl.ds(col_in, BLK)] = from_d[c].astype(f32)
    total[...] = jnp.zeros_like(total)
    lane = lax.broadcasted_iota(jnp.int32, (PATCH, BLK), 1)
    spans = PATCH // BLK
    fetch.wait()

    def place(p):
        u, v = spots[p, 0], spots[p, 1] + (BLK - RIM)
        start = aligned(v // BLK * BLK, BLK)
        top = aligned(u // 8 * 8, 8)
        return top, u - top, start, v - start

    def window(p):
        top, down, start, shift = place(p)
        out = []
        for c in range(2):
            cuts = [frame[c, pl.ds(top, PATCH + 8), pl.ds(aligned(start + k * BLK, BLK), BLK)] for k in range(spans + 1)]
            blocks = [pltpu.roll(rows_from(cut, down), (BLK - shift) % BLK, 1) for cut in cuts]
            keep = lane < BLK - shift
            out.append(
                jnp.concatenate([jnp.where(keep, blocks[k], blocks[k + 1]) for k in range(spans)], axis=1)
            )
        return out

    windows = [window(p) for p in range(patches)]
    for p in range(patches):
        o_re, o_im = windows[p]
        for m in range(modes):
            p_re, p_im = probe[m, 0], probe[m, 1]
            at = slice((p * modes + m) * PATCH, (p * modes + m + 1) * PATCH)
            stack[0:PATCH, at] = (p_re * o_re - p_im * o_im).astype(bf16)
            stack[PATCH:, at] = (p_re * o_im + p_im * o_re).astype(bf16)

    def transform(left, right, p):
        at = slice(p * modes * PATCH, (p + 1) * modes * PATCH)
        half = jnp.dot(dft[left], stack[:, at], preferred_element_type=f32).astype(bf16)
        out = []
        for m in range(modes):
            cut = slice(m * PATCH, (m + 1) * PATCH)
            wide = jnp.concatenate([half[:PATCH, cut], half[PATCH:, cut]], axis=1)
            out.append(jnp.dot(wide, dft[right], preferred_element_type=f32))
        return out

    for p in range(patches):
        far = transform(0, 1, p)
        misfit = sum(f[:, :PATCH] * f[:, :PATCH] + f[:, PATCH:] * f[:, PATCH:] for f in far)
        misfit = misfit - data[p].astype(f32)
        for m in range(modes):
            at = slice((p * modes + m) * PATCH, (p * modes + m + 1) * PATCH)
            stack[0:PATCH, at] = (misfit * far[m][:, :PATCH]).astype(bf16)
            stack[PATCH:, at] = (misfit * far[m][:, PATCH:]).astype(bf16)

    for p in range(patches):
        chi = transform(1, 0, p)
        o_re, o_im = windows[p]
        g_re = g_im = 0.0
        for m in range(modes):
            c_re, c_im = chi[m][:, :PATCH], chi[m][:, PATCH:]
            p_re, p_im = probe[m, 0], probe[m, 1]
            g_re += p_re * c_re + p_im * c_im
            g_im += p_re * c_im - p_im * c_re
            q_re, q_im = o_re * c_re + o_im * c_im, o_re * c_im - o_im * c_re
            for c, q in enumerate((q_re, q_im)):
                q = q + probe_total[m, c] if p else q
                if p < patches - 1:
                    probe_total[m, c] = q
                else:
                    probe_here[m, c] = q.astype(bf16)
        top, down, start, shift = place(p)
        for c, g in enumerate((g_re, g_im)):
            turned = [pltpu.roll(g[:, k * BLK : (k + 1) * BLK], shift, 1) for k in range(spans)]
            none = jnp.zeros_like(turned[0])
            keep = lane >= shift
            for k in range(spans + 1):
                here = turned[k] if k < spans else none
                before = turned[k - 1] if k else none
                to = pl.ds(aligned(start + k * BLK, BLK), BLK)
                total[c, pl.ds(top, PATCH + 8), to] += rows_to(jnp.where(keep, here, before), down)

    out_block = pl.ds(col_in, BLK)
    width = cols + BLK
    for c in range(2):
        for half, wide in ((sx, own), (1 - sx, to_x)):
            wide[c, :, 0:cols] = pick_strips(total, c, RIM, rows, inner, half, h)
            wide[c, :, cols:width] = pick_strips(total, c, RIM, rows, out_block, half, h)
        for half, wide in ((sx, to_y), (1 - sx, to_d)):
            wide[c, :, 0:cols] = pick_strips(total, c, row_in, RIM, inner, half, h)
            wide[c, :, cols:width] = pick_strips(total, c, row_in, RIM, out_block, half, h)
        to_x[c, :, width : width + BLK] = own[c, :, cols:width]


def column_cuts(sx, cols):
    low, high = aligned(sx * cols, BLK), aligned((1 - sx) * cols, BLK)
    edge = cols - BLK
    mine = pl.ds(aligned(sx * edge + (1 - sx) * cols, BLK), BLK)
    other = pl.ds(aligned(sx * cols + (1 - sx) * edge, BLK), BLK)
    return pl.ds(low, cols), pl.ds(high, cols), mine, other


def at_home(group, total, count):
    return lax.axis_index("ang") // group == (1 - lax.axis_index("sy")) * (total - count) // group


def owner_of(first, group, d, k):
    me = lax.axis_index("ang")
    return jnp.where(first, me ^ d ^ (k * group), me ^ d)


def project_kernel(h, group, rims, half, after, own, from_x, weight, chunks, *outs_and_scratch):
    outs, rows_all = outs_and_scratch[:-1], outs_and_scratch[-1]
    sx, me = lax.axis_index("sx"), lax.axis_index("ang")
    f32, bf16 = jnp.float32, jnp.bfloat16
    cols = own.shape[2] - BLK
    total = own.shape[1] // h
    home = at_home(group, total, rims)
    rows = rows_all.shape[1]
    served = 0
    if half is not None:
        served = (me // group) ^ jnp.where(home, 1 - half, half)
    at = pl.ds(aligned(served * rows, rows), rows)
    mine, other, rim_mine, rim_other = column_cuts(sx, cols)
    for c in range(2):
        rows_all[c, :, mine] = own[c, at, 0:cols].astype(f32)
        rows_all[c, :, other] = from_x[c, at, 0:cols].astype(f32)
        rows_all[c, :, rim_mine] += own[c, at, cols:].astype(f32)
        rows_all[c, :, rim_other] += from_x[c, at, cols : cols + BLK].astype(f32)
    stacked = rows_all[...].reshape(2 * rows, 2 * cols).astype(bf16)
    part = jnp.dot(stacked, weight[...], preferred_element_type=f32)
    for c in range(2):
        for j in range(rows // h):
            row = c * rows + j * h
            chunks[j, c * h : (c + 1) * h, :] = part[row : row + h]
    for d, ref in enumerate(outs):
        for k in range(1, total // group):
            owner = owner_of(home, group, d, k) - served * (rows // h)
            ref[(k - 1) * 2 * h : k * 2 * h, :] = chunks[owner].astype(ref.dtype)


def rim_kernel(
    h, group, total, after, from_y, from_d, weight, chunks, *outs_and_scratch
):
    outs, (rows_all, pieces) = outs_and_scratch[:-2], outs_and_scratch[-2:]
    sy, sx = lax.axis_index("sy"), lax.axis_index("sx")
    f32, bf16 = jnp.float32, jnp.bfloat16
    cols = from_y.shape[2] - BLK
    count = from_y.shape[1] // h
    mine, other, rim_mine, rim_other = column_cuts(sx, cols)
    for c in range(2):
        rows_all[c, :, mine] = from_y[c, :, 0:cols].astype(f32)
        rows_all[c, :, other] = from_d[c, :, 0:cols].astype(f32)
        rows_all[c, :, rim_mine] += from_y[c, :, cols:].astype(f32)
        rows_all[c, :, rim_other] += from_d[c, :, cols:].astype(f32)
    rows = rows_all[...].reshape(2 * count * h, 2 * cols).astype(bf16)
    part = jnp.dot(rows, weight[...], preferred_element_type=f32)
    for c in range(2):
        for q in range(count):
            row = (c * count + q) * h
            pieces[q, c * h : (c + 1) * h, :] = part[row : row + h]
    held = chunks.shape[0]
    base = (1 - sy) * (total - count)
    away = jnp.logical_not(at_home(group, total, count))
    for d, ref in enumerate(outs):
        for k in range(1, total // group):
            owner = owner_of(away, group, d, k)
            rel = owner - base
            found = pieces[jnp.clip(rel, 0, count - 1)]
            part = chunks[owner % held] + jnp.where((rel >= 0) & (rel < count), found, jnp.zeros_like(found))
            ref[(k - 1) * 2 * h : k * 2 * h, :] = part.astype(ref.dtype)


def fold_kernel(h, grad, from_x, from_y, from_d, from_core, out):
    sy, sx = lax.axis_index("sy"), lax.axis_index("sx")
    f32 = jnp.float32
    rows, cols = out.shape[1], out.shape[2]
    edge = pl.ds(aligned((1 - sx) * (cols - BLK), BLK), BLK)
    row = aligned((1 - sy) * (rows - RIM), RIM)
    every = pl.ds(0, cols)
    for c in range(2):
        out[c] = grad[c, RIM : RIM + rows, BLK : BLK + cols]
        add_strips(out, c, 0, rows, edge, sx, h, from_x[c, :, cols : cols + BLK].astype(f32))
        add_strips(out, c, 0, rows, edge, 1 - sx, h, from_x[c, :, cols + BLK : cols + 2 * BLK].astype(f32))
        add_strips(out, c, row, RIM, every, sx, h, from_y[c, :, 0:cols].astype(f32))
        add_strips(out, c, row, RIM, edge, sx, h, from_d[c, :, cols:].astype(f32))
        add_strips(out, c, row, RIM, every, 1 - sx, h, from_core[c].astype(f32))


def add(refs):
    total = refs[0][...]
    for ref in refs[1:]:
        total += ref[...].astype(jnp.float32)
    return total


def early_kernel(*refs):
    refs[-1][...] = add(refs[:-1])


def group_kernel(group, total, rims, from_y, from_d, early, *refs):
    late, (across, near, to_core) = refs[:group], refs[group:]
    first, second = early[...], add(late)
    home = at_home(group, total, rims)
    across[...] = jnp.where(home, first, second).astype(across.dtype)
    near[...] = jnp.where(home, second, first)[: near.shape[0]]
    cols = to_core.shape[2]
    edge = pl.ds(aligned(lax.axis_index("sx") * (cols - BLK), BLK), BLK)
    to_core[...] = from_d[:, :, 0:cols]
    at_edge = from_d[:, :, edge].astype(jnp.float32) + from_y[:, :, cols:].astype(jnp.float32)
    to_core[:, :, edge] = at_edge.astype(to_core.dtype)


def probe_sum_kernel(after, kept, received, out):
    out[...] = (kept[...].astype(jnp.float32) + received[...].astype(jnp.float32)).astype(out.dtype)


def last_kernel(h, after, *refs):
    out = refs[-1]
    total = refs[0][...]
    for ref in refs[1:-1]:
        total += ref[...].astype(jnp.float32)
    for c in range(2):
        out[:, c, :] = total[c * h : (c + 1) * h]


def probe_kernel(scale, mine, other, out):
    out[...] = (mine[...].astype(jnp.float32) + other[...].astype(jnp.float32)) * scale


def body(objects, probe, data, positions, block_index, block_values):
    f32, bf16 = jnp.float32, jnp.bfloat16
    obj, measured, pos = objects[0], data[0, 0, 0], positions[0, 0, 0]
    rows, cols = obj.shape[1], obj.shape[2]
    modes, patches = probe.shape[0], measured.shape[0]
    n = lax.axis_size("ang")
    tiles = lax.axis_size("sy") * lax.axis_size("sx")
    h = rows // (n * lax.axis_size("sx"))
    strip_rows = rows // 2
    lines = block_values.shape[0]
    width = lines * BLK
    group = 1
    while group * group < n:
        group *= 2

    to_y, to_x, to_d = call(
        edge_kernel,
        (shape((2, RIM, cols)), shape((2, rows, BLK)), shape((2, RIM, BLK))),
        (obj,), [HBM], [pltpu.SemaphoreType.DMA((3,))], moved=2 * MIB,
    )
    halo_y = lax.ppermute(to_y, "sy", SWAP)
    halo_d = lax.ppermute(to_d, ("sy", "sx"), CROSS)
    halo_x = lax.ppermute(to_x, "sx", SWAP)

    entries = block_index.size // n
    matrix = call(
        partial(gather_kernel, entries),
        shape((width, width)),
        (block_index, block_values),
        [HBM, HBM],
        [
            pltpu.VMEM((entries, BLK, BLK), bf16),
            pltpu.VMEM((entries, BLK, BLK), f32),
            pltpu.SMEM(block_index.shape, jnp.int32),
            pltpu.SMEM((entries + 1,), jnp.int32),
            pltpu.SMEM((lines * lines,), jnp.int32),
            pltpu.SemaphoreType.DMA((entries + 1,)),
        ],
        flops=MIB, moved=4 * MIB,
    )
    carried = (obj, probe, measured, jnp.asarray(dft_blocks(PATCH)))
    weight, obj, probe, measured, dft = call(
        weight_kernel,
        (shape((width, width)),) + tuple(shape(x.shape, x.dtype) for x in carried),
        (matrix, jnp.asarray(ramp_strip(width))) + carried,
        [VMEM, VMEM] + [HBM] * len(carried),
        [pltpu.SemaphoreType.DMA((len(carried),))],
        flops=2 * width**3, moved=6 * MIB,
    )

    wide = cols + BLK
    grad, own, to_x, to_y, to_d, probe_here = call(
        partial(patch_kernel, h),
        (
            shape((2, rows + 2 * RIM + 8, cols + 2 * BLK), f32),
            shape((2, strip_rows, wide)),
            shape((2, strip_rows, wide + BLK)),
            shape((2, RIM // 2, wide)),
            shape((2, RIM // 2, wide)),
            shape((modes, 2, PATCH, PATCH)),
        ),
        (pos, weight, obj, halo_y, halo_x, halo_d, probe, measured, dft),
        [HBM, ANY] + [VMEM] * 7,
        [
            pltpu.VMEM((2, rows + 2 * RIM + 8, cols + 2 * BLK), f32),
            pltpu.VMEM((2 * PATCH, patches * modes * PATCH), bf16),
            pltpu.VMEM((modes, 2, PATCH, PATCH), f32),
            pltpu.SMEM(pos.shape, jnp.int32),
            pltpu.SemaphoreType.DMA,
        ],
        limit=24, flops=patches * modes * 32 * PATCH**3, moved=8 * MIB,
    )

    from_x = lax.ppermute(to_x, "sx", SWAP)
    probe_x = lax.ppermute(probe_here, "sx", SWAP)
    from_y = lax.ppermute(to_y, "sy", SWAP)
    from_d = lax.ppermute(to_d, ("sy", "sx"), CROSS)

    far = n // group - 1
    rims = RIM // (2 * h)
    parts = (shape((far * 2 * h, width), f32),) + (shape((far * 2 * h, width)),) * (group - 1)
    split = far == 1

    def project(half, after, sent):
        rows = strip_rows // 2 if split else strip_rows
        return call(
            partial(project_kernel, h, group, rims, half),
            (shape((rows // h, 2 * h, width), f32),) + sent,
            (after, own, from_x, weight),
            [ANY] + [VMEM] * 3,
            [pltpu.VMEM((2, rows, width), f32)],
            flops=4 * rows * width * width, moved=8 * MIB,
        )

    chunks, *early = project(0 if split else None, weight, parts)
    if split:
        (chunks,) = project(1, chunks, ())
    probe_here = call(
        probe_sum_kernel, shape((modes, 2, PATCH, PATCH)), (early[0], probe_here, probe_x),
        [ANY, VMEM, VMEM], moved=MIB,
    )
    late = call(
        partial(rim_kernel, h, group, n),
        parts,
        (probe_here, from_y, from_d, weight, chunks),
        [ANY] + [VMEM] * 4,
        [pltpu.VMEM((2, RIM // 2, width), f32), pltpu.VMEM((rims, 2 * h, width), f32)],
        flops=12 * width**3, moved=4 * MIB,
    )

    def swap(array, d):
        return lax.ppermute(array, "ang", [(i, i ^ d) for i in range(n)])

    order = range(1, group)
    late_here, late = late[0], list(late)
    early[1:] = [swap(early[d], d) for d in order]
    late[1:] = [swap(late[d], d) for d in order]
    early = call(early_kernel, parts[0], early, [VMEM] * group, flops=16 * width**3 // 4, moved=MIB)
    across, near, to_core = call(
        partial(group_kernel, group, n, rims),
        (shape((far * 2 * h, width)), shape((2 * h, width), f32), shape((2, RIM // 2, cols))),
        [from_y, from_d, early] + late, [VMEM] * (3 + group), moved=MIB,
    )
    across_got = [swap(across[(k - 1) * 2 * h : k * 2 * h], k * group) for k in range(1, far + 1)]

    probe_y = lax.ppermute(probe_here, "sy", SWAP)
    from_core = lax.ppermute(to_core, "sx", SWAP)
    object_grad = call(
        partial(fold_kernel, h),
        shape((2, rows, cols), f32),
        (grad, from_x, from_y, from_d, from_core),
        [VMEM] * 5, moved=6 * MIB,
    )
    probe_grad = call(
        partial(probe_kernel, 1.0 / math.sqrt(patches * tiles)),
        shape((modes, 2, PATCH, PATCH), f32),
        (probe_here, probe_y),
        [VMEM] * 2, moved=2 * MIB,
    )
    vol = call(
        partial(last_kernel, h),
        shape((h, 2, width), f32),
        [probe_grad, near] + across_got,
        [HBM] + [VMEM] * (1 + far), moved=MIB,
    )
    return (object_grad[None], probe_grad[None], vol[None])


def solution(mesh):
    placed = (
        P("ang", None, "sy", "sx"),
        P(),
        P("ang", "sy", "sx", None, None, None),
        P("ang", "sy", "sx", None, None),
        P(),
        P(),
    )
    return jax.shard_map(
        body,
        mesh=mesh,
        in_specs=placed,
        out_specs=(
            P("ang", None, "sy", "sx"),
            P("ang", None, None, None, None),
            P("sy", ("ang", "sx"), None, None),
        ),
        check_vma=False,
    )
```

```python
from functools import partial
import math

import jax
import jax.numpy as jnp
import ml_dtypes
import numpy as np
from jax import lax
from jax.experimental import pallas as pl
from jax.experimental.pallas import tpu as pltpu
from jax.sharding import PartitionSpec as P

PATCH = 256
RIM = 64
BLK = 128
SWAP = [(0, 1), (1, 0)]
CROSS = [(0, 3), (3, 0), (1, 2), (2, 1)]
MIB = 1 << 20

VMEM = pl.BlockSpec(memory_space=pltpu.VMEM)
SMEM = pl.BlockSpec(memory_space=pltpu.SMEM)
ANY = pl.BlockSpec(memory_space=pl.ANY)
HBM = pl.BlockSpec(memory_space=pltpu.HBM)


def dft_blocks(length):
    ids = np.arange(length)
    phases = (ids[:, None] * ids[None, :] % length) * (2.0 * math.pi / length)
    factor = 1.0 / math.sqrt(length)
    re, im = np.cos(phases) * factor, -np.sin(phases) * factor
    forward = np.block([[re, -im], [im, re]])
    backward = np.block([[re, im], [-im, re]])
    return np.stack([forward, backward]).astype(np.float32).astype(ml_dtypes.bfloat16)


def ramp_strip(width):
    offsets = np.arange(2 * width - BLK)[None, :] - (width - BLK) - np.arange(BLK)[:, None]
    scaled = offsets.astype(np.float64) * math.pi
    values = np.where(offsets % 2 != 0, -1.0 / np.maximum(scaled * scaled, 1.0), 0.0)
    values = np.where(offsets == 0, 0.25, values)
    return values.astype(np.float32).astype(ml_dtypes.bfloat16)


def shape(dims, dtype=jnp.bfloat16):
    return jax.ShapeDtypeStruct(dims, dtype)


def call(kernel, outs, ins, specs, scratch=(), limit=16, flops=0, moved=0):
    ins = [
        pltpu.with_memory_space_constraint(x, pltpu.HBM) if spec is HBM else x
        for x, spec in zip(ins, specs, strict=True)
    ]
    return pl.pallas_call(
        kernel,
        out_shape=outs,
        in_specs=specs,
        out_specs=jax.tree.map(lambda _: VMEM, outs),
        scratch_shapes=list(scratch),
        compiler_params=pltpu.CompilerParams(vmem_limit_bytes=limit * MIB),
        cost_estimate=pl.CostEstimate(flops=flops, bytes_accessed=moved, transcendentals=0),
    )(*ins)


def aligned(value, step):
    return pl.multiple_of(value, step)


def edge_kernel(obj, to_y, to_x, to_d, sems):
    sy, sx = lax.axis_index("sy"), lax.axis_index("sx")
    rows, cols = obj.shape[1], obj.shape[2]
    r = pl.ds(aligned((1 - sy) * (rows - RIM), RIM), RIM)
    c = pl.ds(aligned((1 - sx) * (cols - BLK), BLK), BLK)
    copies = [
        pltpu.make_async_copy(obj.at[:, r, :], to_y, sems.at[0]),
        pltpu.make_async_copy(obj.at[:, r, c], to_d, sems.at[1]),
        pltpu.make_async_copy(obj.at[:, :, c], to_x, sems.at[2]),
    ]
    for copy in copies:
        copy.start()
    for copy in copies:
        copy.wait()


def gather_kernel(count, index, values, out, blocks, sums, index_here, found, slots, sems):
    me = lax.axis_index("ang")
    lines, per = index.shape
    first = pltpu.make_async_copy(index, index_here, sems.at[count])
    first.start()
    out[...] = jnp.zeros_like(out)
    for i in range(lines * lines):
        slots[i] = jnp.int32(count)
    first.wait()
    low, high = me * lines, (me + 1) * lines
    n = jnp.int32(0)
    for b in range(lines):
        for k in range(per):
            g = index_here[b, k]
            found[n] = jnp.int32(b * per + k)
            n = jnp.minimum(n + ((g >= low) & (g < high)).astype(jnp.int32), count)
    copies, places = [], []
    for i in range(count):
        e = found[i]
        b, k = lax.div(e, per), lax.rem(e, per)
        copies.append(pltpu.make_async_copy(values.at[b, k], blocks.at[i], sems.at[i]))
        copies[i].start()
        places.append((index_here[b, k] - low, b))
    for copy in copies:
        copy.wait()
    for i, (line, b) in enumerate(places):
        place = line * lines + b
        slot = jnp.minimum(slots[place], i)
        value = blocks[i].astype(jnp.float32)
        sums[slot] = jnp.where(slot < i, sums[slot] + value, value)
        slots[place] = slot
        row, col = pl.ds(aligned(line * BLK, BLK), BLK), pl.ds(aligned(b * BLK, BLK), BLK)
        out[row, col] = sums[slot].astype(out.dtype)


def weight_kernel(matrix, strip, *refs):
    steps = (len(refs) - 2) // 2
    sources, out, targets, sems = refs[:steps], refs[steps], refs[steps + 1 : -1], refs[-1]
    moves = [
        pltpu.make_async_copy(source, target, sems.at[i])
        for i, (source, target) in enumerate(zip(sources, targets, strict=True))
    ]
    for move in moves:
        move.start()
    width = out.shape[0]
    starts = range(width - BLK, -1, -BLK)
    ramp = jnp.concatenate([strip[:, start : start + width] for start in starts], axis=0)
    out[...] = jnp.dot(ramp, matrix[...], preferred_element_type=jnp.float32).astype(out.dtype)
    for move in moves:
        move.wait()


def strip_select(half, rows, h, dtype):
    i = lax.broadcasted_iota(jnp.int32, (rows // 2, rows), 0)
    j = lax.broadcasted_iota(jnp.int32, (rows // 2, rows), 1)
    return (j == i // h * 2 * h + half * h + i % h).astype(dtype)


def pick_strips(ref, c, row, rows, lanes, half, h):
    if h % 8 == 0:
        parts = [
            ref[c, pl.ds(aligned(row + q * 2 * h + half * h, 8), h), lanes]
            for q in range(rows // (2 * h))
        ]
        return jnp.concatenate(parts, axis=0).astype(jnp.bfloat16)
    whole = ref[c, pl.ds(aligned(row, 8), rows), lanes].astype(jnp.bfloat16)
    chosen = strip_select(half, rows, h, jnp.bfloat16)
    return jnp.dot(chosen, whole, preferred_element_type=jnp.float32).astype(jnp.bfloat16)


def add_strips(ref, c, row, rows, lanes, half, h, terms):
    if h % 8 == 0:
        for q in range(rows // (2 * h)):
            at = pl.ds(aligned(row + q * 2 * h + half * h, 8), h)
            ref[c, at, lanes] += terms[q * h : (q + 1) * h]
        return
    chosen = strip_select(half, rows, h, jnp.float32)
    at = pl.ds(aligned(row, 8), rows)
    ref[c, at, lanes] += lax.dot_general(
        chosen, terms, (((0,), (0,)), ((), ())), precision=lax.Precision.HIGHEST,
        preferred_element_type=jnp.float32,
    )


def rows_from(value, shift):
    rows, lanes = value.shape[0] - 8, value.shape[1]
    turned = pltpu.roll(value.reshape(rows // 8 + 1, 8, lanes), (8 - shift) % 8, 1)
    keep = lax.broadcasted_iota(jnp.int32, (rows // 8, 8, lanes), 1) < 8 - shift
    return jnp.where(keep, turned[:-1], turned[1:]).reshape(rows, lanes)


def rows_to(value, shift):
    rows, lanes = value.shape
    turned = pltpu.roll(value.reshape(rows // 8, 8, lanes), shift, 1)
    none = jnp.zeros((1, 8, lanes), value.dtype)
    keep = lax.broadcasted_iota(jnp.int32, (rows // 8 + 1, 8, lanes), 1) >= shift
    here = jnp.concatenate([turned, none], axis=0)
    before = jnp.concatenate([none, turned], axis=0)
    return jnp.where(keep, here, before).reshape(rows + 8, lanes)


def patch_kernel(
    h, pos, ahead, obj, from_y, from_x, from_d, probe, data, dft,
    total, own, to_x, to_y, to_d, probe_here,
    frame, stack, probe_total, spots, sem,
):
    fetch = pltpu.make_async_copy(pos, spots, sem)
    fetch.start()
    sy, sx = lax.axis_index("sy"), lax.axis_index("sx")
    rows, cols = obj.shape[1], obj.shape[2]
    modes = probe.shape[0]
    patches = data.shape[0]
    f32, bf16 = jnp.float32, jnp.bfloat16
    last = RIM + rows
    row_in = aligned((1 - sy) * last, RIM)
    row_out = aligned(sy * last, RIM)
    col_in = aligned((1 - sx) * (BLK + cols), BLK)
    col_out = aligned(sx * (BLK + cols), BLK)
    inner = pl.ds(BLK, cols)
    for c in range(2):
        frame[c, RIM:last, BLK : BLK + cols] = obj[c].astype(f32)
        frame[c, pl.ds(row_out, RIM), :] = jnp.zeros((RIM, frame.shape[2]), f32)
        frame[c, :, pl.ds(col_out, BLK)] = jnp.zeros((frame.shape[1], BLK), f32)
        frame[c, RIM:last, pl.ds(col_in, BLK)] = from_x[c].astype(f32)
        frame[c, pl.ds(row_in, RIM), inner] = from_y[c].astype(f32)
        frame[c, pl.ds(row_in, RIM), pl.ds(col_in, BLK)] = from_d[c].astype(f32)
    total[...] = jnp.zeros_like(total)
    lane = lax.broadcasted_iota(jnp.int32, (PATCH, BLK), 1)
    spans = PATCH // BLK
    fetch.wait()

    def place(p):
        u, v = spots[p, 0], spots[p, 1] + (BLK - RIM)
        start = aligned(v // BLK * BLK, BLK)
        top = aligned(u // 8 * 8, 8)
        return top, u - top, start, v - start

    def window(p):
        top, down, start, shift = place(p)
        out = []
        for c in range(2):
            cuts = [frame[c, pl.ds(top, PATCH + 8), pl.ds(aligned(start + k * BLK, BLK), BLK)] for k in range(spans + 1)]
            blocks = [pltpu.roll(rows_from(cut, down), (BLK - shift) % BLK, 1) for cut in cuts]
            keep = lane < BLK - shift
            out.append(
                jnp.concatenate([jnp.where(keep, blocks[k], blocks[k + 1]) for k in range(spans)], axis=1)
            )
        return out

    windows = [window(p) for p in range(patches)]
    for p in range(patches):
        o_re, o_im = windows[p]
        for m in range(modes):
            p_re, p_im = probe[m, 0], probe[m, 1]
            at = slice((p * modes + m) * PATCH, (p * modes + m + 1) * PATCH)
            stack[0:PATCH, at] = (p_re * o_re - p_im * o_im).astype(bf16)
            stack[PATCH:, at] = (p_re * o_im + p_im * o_re).astype(bf16)

    def transform(left, right, p):
        at = slice(p * modes * PATCH, (p + 1) * modes * PATCH)
        half = jnp.dot(dft[left], stack[:, at], preferred_element_type=f32).astype(bf16)
        out = []
        for m in range(modes):
            cut = slice(m * PATCH, (m + 1) * PATCH)
            wide = jnp.concatenate([half[:PATCH, cut], half[PATCH:, cut]], axis=1)
            out.append(jnp.dot(wide, dft[right], preferred_element_type=f32))
        return out

    for p in range(patches):
        far = transform(0, 1, p)
        misfit = sum(f[:, :PATCH] * f[:, :PATCH] + f[:, PATCH:] * f[:, PATCH:] for f in far)
        misfit = misfit - data[p].astype(f32)
        for m in range(modes):
            at = slice((p * modes + m) * PATCH, (p * modes + m + 1) * PATCH)
            stack[0:PATCH, at] = (misfit * far[m][:, :PATCH]).astype(bf16)
            stack[PATCH:, at] = (misfit * far[m][:, PATCH:]).astype(bf16)

    for p in range(patches):
        chi = transform(1, 0, p)
        o_re, o_im = windows[p]
        g_re = g_im = 0.0
        for m in range(modes):
            c_re, c_im = chi[m][:, :PATCH], chi[m][:, PATCH:]
            p_re, p_im = probe[m, 0], probe[m, 1]
            g_re += p_re * c_re + p_im * c_im
            g_im += p_re * c_im - p_im * c_re
            q_re, q_im = o_re * c_re + o_im * c_im, o_re * c_im - o_im * c_re
            for c, q in enumerate((q_re, q_im)):
                q = q + probe_total[m, c] if p else q
                if p < patches - 1:
                    probe_total[m, c] = q
                else:
                    probe_here[c, :, m * PATCH : (m + 1) * PATCH] = q.astype(bf16)
        top, down, start, shift = place(p)
        for c, g in enumerate((g_re, g_im)):
            turned = [pltpu.roll(g[:, k * BLK : (k + 1) * BLK], shift, 1) for k in range(spans)]
            none = jnp.zeros_like(turned[0])
            keep = lane >= shift
            for k in range(spans + 1):
                here = turned[k] if k < spans else none
                before = turned[k - 1] if k else none
                to = pl.ds(aligned(start + k * BLK, BLK), BLK)
                total[c, pl.ds(top, PATCH + 8), to] += rows_to(jnp.where(keep, here, before), down)

    out_block = pl.ds(col_in, BLK)
    width = cols + BLK
    for c in range(2):
        for half, wide in ((sx, own), (1 - sx, to_x)):
            wide[c, :, 0:cols] = pick_strips(total, c, RIM, rows, inner, half, h)
            wide[c, :, cols:width] = pick_strips(total, c, RIM, rows, out_block, half, h)
        for half, wide in ((sx, to_y), (1 - sx, to_d)):
            wide[c, :, 0:cols] = pick_strips(total, c, row_in, RIM, inner, half, h)
            wide[c, :, cols:width] = pick_strips(total, c, row_in, RIM, out_block, half, h)
        probe_here[c, :, modes * PATCH :] = own[c, :, cols:width]


def column_cuts(sx, cols):
    low, high = aligned(sx * cols, BLK), aligned((1 - sx) * cols, BLK)
    edge = cols - BLK
    mine = pl.ds(aligned(sx * edge + (1 - sx) * cols, BLK), BLK)
    other = pl.ds(aligned(sx * cols + (1 - sx) * edge, BLK), BLK)
    return pl.ds(low, cols), pl.ds(high, cols), mine, other


def at_home(group, total, count):
    return lax.axis_index("ang") // group == (1 - lax.axis_index("sy")) * (total - count) // group


def owner_of(first, group, d, k):
    me = lax.axis_index("ang")
    return jnp.where(first, me ^ d ^ (k * group), me ^ d)


def project_kernel(h, group, rims, half, after, own, from_x, weight, chunks, *outs_and_scratch):
    outs, rows_all = outs_and_scratch[:-1], outs_and_scratch[-1]
    sx, me = lax.axis_index("sx"), lax.axis_index("ang")
    f32, bf16 = jnp.float32, jnp.bfloat16
    cols = own.shape[2] - BLK
    total = own.shape[1] // h
    home = at_home(group, total, rims)
    rows = rows_all.shape[1]
    served = 0
    if half is not None:
        served = (me // group) ^ jnp.where(home, 1 - half, half)
    at = pl.ds(aligned(served * rows, rows), rows)
    mine, other, rim_mine, rim_other = column_cuts(sx, cols)
    for c in range(2):
        rows_all[c, :, mine] = own[c, at, 0:cols].astype(f32)
        rows_all[c, :, other] = from_x[c, at, 0:cols].astype(f32)
        rows_all[c, :, rim_mine] += own[c, at, cols:].astype(f32)
        rows_all[c, :, rim_other] += from_x[c, at, cols : cols + BLK].astype(f32)
    stacked = rows_all[...].reshape(2 * rows, 2 * cols).astype(bf16)
    part = jnp.dot(stacked, weight[...], preferred_element_type=f32)
    for c in range(2):
        for j in range(rows // h):
            row = c * rows + j * h
            chunks[j, c * h : (c + 1) * h, :] = part[row : row + h]
    for d, ref in enumerate(outs):
        for k in range(1, total // group):
            owner = owner_of(home, group, d, k) - served * (rows // h)
            ref[(k - 1) * 2 * h : k * 2 * h, :] = chunks[owner].astype(ref.dtype)


def rim_kernel(
    h, group, total, after, from_y, from_d, weight, chunks, *outs_and_scratch
):
    outs, (rows_all, pieces) = outs_and_scratch[:-2], outs_and_scratch[-2:]
    sy, sx = lax.axis_index("sy"), lax.axis_index("sx")
    f32, bf16 = jnp.float32, jnp.bfloat16
    cols = from_y.shape[2] - BLK
    count = from_y.shape[1] // h
    mine, other, rim_mine, rim_other = column_cuts(sx, cols)
    for c in range(2):
        rows_all[c, :, mine] = from_y[c, :, 0:cols].astype(f32)
        rows_all[c, :, other] = from_d[c, :, 0:cols].astype(f32)
        rows_all[c, :, rim_mine] += from_y[c, :, cols:].astype(f32)
        rows_all[c, :, rim_other] += from_d[c, :, cols:].astype(f32)
    rows = rows_all[...].reshape(2 * count * h, 2 * cols).astype(bf16)
    part = jnp.dot(rows, weight[...], preferred_element_type=f32)
    for c in range(2):
        for q in range(count):
            row = (c * count + q) * h
            pieces[q, c * h : (c + 1) * h, :] = part[row : row + h]
    held = chunks.shape[0]
    base = (1 - sy) * (total - count)
    away = jnp.logical_not(at_home(group, total, count))
    for d, ref in enumerate(outs):
        for k in range(1, total // group):
            owner = owner_of(away, group, d, k)
            rel = owner - base
            found = pieces[jnp.clip(rel, 0, count - 1)]
            part = chunks[owner % held] + jnp.where((rel >= 0) & (rel < count), found, jnp.zeros_like(found))
            ref[(k - 1) * 2 * h : k * 2 * h, :] = part.astype(ref.dtype)


def fold_kernel(h, grad, from_x, rim_x, from_y, from_d, from_core, out):
    sy, sx = lax.axis_index("sy"), lax.axis_index("sx")
    f32 = jnp.float32
    rows, cols = out.shape[1], out.shape[2]
    edge = pl.ds(aligned((1 - sx) * (cols - BLK), BLK), BLK)
    row = aligned((1 - sy) * (rows - RIM), RIM)
    every = pl.ds(0, cols)
    for c in range(2):
        out[c] = grad[c, RIM : RIM + rows, BLK : BLK + cols]
        add_strips(out, c, 0, rows, edge, sx, h, from_x[c, :, cols : cols + BLK].astype(f32))
        add_strips(out, c, 0, rows, edge, 1 - sx, h, rim_x[c, :, rim_x.shape[2] - BLK :].astype(f32))
        add_strips(out, c, row, RIM, every, sx, h, from_y[c, :, 0:cols].astype(f32))
        add_strips(out, c, row, RIM, edge, sx, h, from_d[c, :, cols:].astype(f32))
        add_strips(out, c, row, RIM, every, 1 - sx, h, from_core[c].astype(f32))


def add(refs):
    total = refs[0][...]
    for ref in refs[1:]:
        total += ref[...].astype(jnp.float32)
    return total


def early_kernel(*refs):
    refs[-1][...] = add(refs[:-1])


def group_kernel(group, total, rims, from_y, from_d, early, *refs):
    late, (across, near, to_core) = refs[:group], refs[group:]
    first, second = early[...], add(late)
    home = at_home(group, total, rims)
    across[...] = jnp.where(home, first, second).astype(across.dtype)
    near[...] = jnp.where(home, second, first)[: near.shape[0]]
    cols = to_core.shape[2]
    edge = pl.ds(aligned(lax.axis_index("sx") * (cols - BLK), BLK), BLK)
    to_core[...] = from_d[:, :, 0:cols]
    at_edge = from_d[:, :, edge].astype(jnp.float32) + from_y[:, :, cols:].astype(jnp.float32)
    to_core[:, :, edge] = at_edge.astype(to_core.dtype)


def probe_sum_kernel(after, kept, received, out):
    for m in range(out.shape[0]):
        at = slice(m * PATCH, (m + 1) * PATCH)
        total = kept[:, :, at].astype(jnp.float32) + received[:, :, at].astype(jnp.float32)
        out[m] = total.astype(out.dtype)


def last_kernel(h, after, *refs):
    out = refs[-1]
    total = refs[0][...]
    for ref in refs[1:-1]:
        total += ref[...].astype(jnp.float32)
    for c in range(2):
        out[:, c, :] = total[c * h : (c + 1) * h]


def probe_kernel(scale, mine, other, out):
    out[...] = (mine[...].astype(jnp.float32) + other[...].astype(jnp.float32)) * scale


def body(objects, probe, data, positions, block_index, block_values):
    f32, bf16 = jnp.float32, jnp.bfloat16
    obj, measured, pos = objects[0], data[0, 0, 0], positions[0, 0, 0]
    rows, cols = obj.shape[1], obj.shape[2]
    modes, patches = probe.shape[0], measured.shape[0]
    n = lax.axis_size("ang")
    tiles = lax.axis_size("sy") * lax.axis_size("sx")
    h = rows // (n * lax.axis_size("sx"))
    strip_rows = rows // 2
    lines = block_values.shape[0]
    width = lines * BLK
    group = 1
    while group * group < n:
        group *= 2

    to_y, to_x, to_d = call(
        edge_kernel,
        (shape((2, RIM, cols)), shape((2, rows, BLK)), shape((2, RIM, BLK))),
        (obj,), [HBM], [pltpu.SemaphoreType.DMA((3,))], moved=2 * MIB,
    )
    halo_y = lax.ppermute(to_y, "sy", SWAP)
    halo_d = lax.ppermute(to_d, ("sy", "sx"), CROSS)
    halo_x = lax.ppermute(to_x, "sx", SWAP)

    entries = block_index.size // n
    matrix = call(
        partial(gather_kernel, entries),
        shape((width, width)),
        (block_index, block_values),
        [HBM, HBM],
        [
            pltpu.VMEM((entries, BLK, BLK), bf16),
            pltpu.VMEM((entries, BLK, BLK), f32),
            pltpu.SMEM(block_index.shape, jnp.int32),
            pltpu.SMEM((entries + 1,), jnp.int32),
            pltpu.SMEM((lines * lines,), jnp.int32),
            pltpu.SemaphoreType.DMA((entries + 1,)),
        ],
        flops=MIB, moved=4 * MIB,
    )
    carried = (obj, probe, measured, jnp.asarray(dft_blocks(PATCH)))
    weight, obj, probe, measured, dft = call(
        weight_kernel,
        (shape((width, width)),) + tuple(shape(x.shape, x.dtype) for x in carried),
        (matrix, jnp.asarray(ramp_strip(width))) + carried,
        [VMEM, VMEM] + [HBM] * len(carried),
        [pltpu.SemaphoreType.DMA((len(carried),))],
        flops=2 * width**3, moved=6 * MIB,
    )

    wide = cols + BLK
    grad, own, to_x, to_y, to_d, probe_here = call(
        partial(patch_kernel, h),
        (
            shape((2, rows + 2 * RIM + 8, cols + 2 * BLK), f32),
            shape((2, strip_rows, wide)),
            shape((2, strip_rows, wide)),
            shape((2, RIM // 2, wide)),
            shape((2, RIM // 2, wide)),
            shape((2, PATCH, modes * PATCH + BLK)),
        ),
        (pos, weight, obj, halo_y, halo_x, halo_d, probe, measured, dft),
        [HBM, ANY] + [VMEM] * 7,
        [
            pltpu.VMEM((2, rows + 2 * RIM + 8, cols + 2 * BLK), f32),
            pltpu.VMEM((2 * PATCH, patches * modes * PATCH), bf16),
            pltpu.VMEM((modes, 2, PATCH, PATCH), f32),
            pltpu.SMEM(pos.shape, jnp.int32),
            pltpu.SemaphoreType.DMA,
        ],
        limit=24, flops=patches * modes * 32 * PATCH**3, moved=8 * MIB,
    )

    from_x = lax.ppermute(to_x, "sx", SWAP)
    probe_x = lax.ppermute(probe_here, "sx", SWAP)
    from_y = lax.ppermute(to_y, "sy", SWAP)
    from_d = lax.ppermute(to_d, ("sy", "sx"), CROSS)

    far = n // group - 1
    rims = RIM // (2 * h)
    parts = (shape((far * 2 * h, width), f32),) + (shape((far * 2 * h, width)),) * (group - 1)
    split = far == 1

    def project(half, after, sent):
        rows = strip_rows // 2 if split else strip_rows
        return call(
            partial(project_kernel, h, group, rims, half),
            (shape((rows // h, 2 * h, width), f32),) + sent,
            (after, own, from_x, weight),
            [ANY] + [VMEM] * 3,
            [pltpu.VMEM((2, rows, width), f32)],
            flops=4 * rows * width * width, moved=8 * MIB,
        )

    chunks, *early = project(0 if split else None, weight, parts)
    if split:
        (chunks,) = project(1, chunks, ())
    probe_here = call(
        probe_sum_kernel, shape((modes, 2, PATCH, PATCH)), (early[0], probe_here, probe_x),
        [ANY, VMEM, VMEM], moved=MIB,
    )
    late = call(
        partial(rim_kernel, h, group, n),
        parts,
        (probe_here, from_y, from_d, weight, chunks),
        [ANY] + [VMEM] * 4,
        [pltpu.VMEM((2, RIM // 2, width), f32), pltpu.VMEM((rims, 2 * h, width), f32)],
        flops=12 * width**3, moved=4 * MIB,
    )

    def swap(array, d):
        return lax.ppermute(array, "ang", [(i, i ^ d) for i in range(n)])

    order = range(1, group)
    late_here, late = late[0], list(late)
    early[1:] = [swap(early[d], d) for d in order]
    late[1:] = [swap(late[d], d) for d in order]
    early = call(early_kernel, parts[0], early, [VMEM] * group, flops=16 * width**3 // 4, moved=MIB)
    across, near, to_core = call(
        partial(group_kernel, group, n, rims),
        (shape((far * 2 * h, width)), shape((2 * h, width), f32), shape((2, RIM // 2, cols))),
        [from_y, from_d, early] + late, [VMEM] * (3 + group), moved=MIB,
    )
    across_got = [swap(across[(k - 1) * 2 * h : k * 2 * h], k * group) for k in range(1, far + 1)]

    probe_y = lax.ppermute(probe_here, "sy", SWAP)
    from_core = lax.ppermute(to_core, "sx", SWAP)
    object_grad = call(
        partial(fold_kernel, h),
        shape((2, rows, cols), f32),
        (grad, from_x, probe_x, from_y, from_d, from_core),
        [VMEM] * 6, moved=6 * MIB,
    )
    probe_grad = call(
        partial(probe_kernel, 1.0 / math.sqrt(patches * tiles)),
        shape((modes, 2, PATCH, PATCH), f32),
        (probe_here, probe_y),
        [VMEM] * 2, moved=2 * MIB,
    )
    vol = call(
        partial(last_kernel, h),
        shape((h, 2, width), f32),
        [probe_grad, near] + across_got,
        [HBM] + [VMEM] * (1 + far), moved=MIB,
    )
    return (object_grad[None], probe_grad[None], vol[None])


def solution(mesh):
    placed = (
        P("ang", None, "sy", "sx"),
        P(),
        P("ang", "sy", "sx", None, None, None),
        P("ang", "sy", "sx", None, None),
        P(),
        P(),
    )
    return jax.shard_map(
        body,
        mesh=mesh,
        in_specs=placed,
        out_specs=(
            P("ang", None, "sy", "sx"),
            P("ang", None, None, None, None),
            P("sy", ("ang", "sx"), None, None),
        ),
        check_vma=False,
    )
```
